128 devices in a mesh: freq: 8 (over x, core), slab: 16 (over y, z).
Axes of the slice: x: 4, y: 4, z: 4, core: 2. Of those that a mesh axis runs over, the one named last changes fastest.
Arguments:
- traces: bfloat16 [393216, 2048], P(('freq', 'slab')), may hold values from -6 to 6
- trace_counts: int32 [128, 8], P(('freq', 'slab')), may hold values from 1 to 512, 3072 in all within a row
- aperture_start: int32 [1024], P(('freq', 'slab')), may hold values from 0 to 511
- shot_position: int32 [1024], P(('freq', 'slab')), may hold values from 0 to 4095
- rec_slot: int32 [512], replicated, may hold values from 0 to 767, as said below
Outputs:
- encoded: bfloat16 [768, 256, 256], P('slab', 'freq')
The draws below stay inside these ranges and needn't reach their ends.
Inputs may be any that keep to these rules, and one draw needn't show every extreme that they name: `rec_slot`: distinct receivers have distinct slots. No depth slab owns more than 48 receivers, at least one owns exactly 48, and slots 0 and 767 are always used.
All inputs are finite; a program needn't handle non-finite values.
Results may differ from the reference program's by a relative error of at most 0.0062.
Values may be sent and summed in bfloat16 or wider, within the bound.
No kernel may reach another device: no remote copies, remote signals or barrier semaphores. Data moves between devices by JAX's collectives and lax.ppermute only.
A program may use at most 192 MiB of HBM per device.

```python
import math
import jax
import jax.numpy as jnp
import numpy as np
from jax import lax

NT = 2048
FREQUENCY_COUNT = 256
F0 = 8
RAY_PARAM_COUNT = 128
NREC = 512
NXS = 4096
RDIV = 16
ROW_DEV = 3072
SHOTS_PER_UNIT = 8
SHOTS = 1024
ROWS = 393216
SLAB_SLOT_LIMIT = 48
TOTAL_SLOTS = 768
DEVICES = 128


def draw_rec_slot(key, part):
    owner_of_key, score_of_key, key_order = jax.random.split(key, 3)
    complete_owner_table = jax.random.randint(owner_of_key, (), 0, TOTAL_SLOTS // SLAB_SLOT_LIMIT)
    receiver_slot_index = jnp.arange(TOTAL_SLOTS, dtype=jnp.int32)
    ranking_scores = jax.random.randint(score_of_key, (TOTAL_SLOTS,), 0, 1 << 20) * TOTAL_SLOTS + receiver_slot_index
    pinned_choice = (receiver_slot_index // SLAB_SLOT_LIMIT == complete_owner_table) | (receiver_slot_index == 0) | (receiver_slot_index == TOTAL_SLOTS - 1)
    ranking_scores = jnp.where(pinned_choice, ranking_scores + (1 << 30), ranking_scores)
    unused, chosen = lax.top_k(ranking_scores, NREC)
    shuffle = jax.random.permutation(key_order, NREC)
    return chosen[shuffle].astype(jnp.int32)


def set_ends(array, own_key, low, top_value):
    dims = array.shape
    spot = [jax.random.randint(jax.random.fold_in(own_key, axis), (), 0, dims[axis]) for axis in range(len(dims))]
    array = array.at[tuple(spot)].set(low)
    longest = dims.index(max(dims))
    spot[longest] = (spot[longest] + 1) % dims[longest]
    return array.at[tuple(spot)].set(top_value)


def levels(stream_key, shape, cuts, least, largest):
    loudness = 1.0
    for position, blocks in cuts:
        heights = jax.random.uniform(jax.random.fold_in(jax.random.fold_in(stream_key, 6), position), (blocks,), jnp.float32, least / len(cuts), largest / len(cuts))
        loudness = loudness * jnp.repeat(jnp.exp(heights), shape[position] // blocks).reshape((-1,) + (1,) * (len(shape) - 1 - position))
    return loudness


def profile(count, total, limit, skew):
    loads = [(1 << 20) // math.isqrt(grade ** skew) + 1 for grade in range(2, count + 1)]
    rest, given = total - limit - (count - 1), [1] * (count - 1)
    while rest > 0:
        candidates = [i for i in range(count - 1) if given[i] < limit]
        pool, budget = sum([loads[i] for i in candidates]), rest
        for i in candidates:
            addition = min(limit - given[i], max(1, budget * loads[i] // pool), rest)
            given[i] = given[i] + addition
            rest = rest - addition
    return np.array([limit] + given)


def ragged_sizes(key, amount, total, most, slope):
    if amount == 2:
        one = jax.random.randint(key, (), max(1, total - most), min(most, total - 1) + 1)
        return jnp.stack([one, total - one])
    sizes = jnp.asarray(profile(amount, total, most, slope), jnp.int32)
    pairs = (amount - 1) // 2
    giver, taker = sizes[1:1 + 2 * pairs:2], sizes[2:2 + 2 * pairs:2]
    slack = jnp.minimum(giver - 1, most - taker)
    moved = jax.random.randint(jax.random.fold_in(key, 1), (pairs,), 0, 1 << 20) % (slack + 1)
    sizes = sizes.at[1:1 + 2 * pairs:2].set(giver - moved).at[2:2 + 2 * pairs:2].set(taker + moved)
    return sizes[jax.random.permutation(jax.random.fold_in(key, 2), amount)]


def gaussian(own_key, shape, spread, reach, cuts=(), kind=jnp.bfloat16):
    factor_of = levels(own_key, shape, cuts, -0.22, 0.18) if cuts else 1.0
    array = jax.random.normal(own_key, shape, jnp.float32) * spread * factor_of
    return jnp.minimum(jnp.maximum(array, -reach), reach).astype(kind)


def setup_inputs(seed: int = 0) -> dict:
    streams_of = jax.random.split(jax.random.key(seed), 6)
    return {
        "traces": gaussian(streams_of[0], (ROWS, NT), 1.0, 6.0, ((0, 128),)),
        "trace_counts": jax.vmap(lambda own: ragged_sizes(own, SHOTS_PER_UNIT, ROW_DEV, NREC, 2))(jax.random.split(streams_of[1], DEVICES)).reshape((DEVICES, SHOTS_PER_UNIT)).astype(jnp.int32),
        "aperture_start": set_ends(jax.random.randint(streams_of[2], (SHOTS,), 0, NREC), jax.random.fold_in(streams_of[2], 1), 0, NREC - 1).astype(jnp.int32),
        "shot_position": set_ends(jax.random.randint(streams_of[3], (SHOTS,), 0, NXS), jax.random.fold_in(streams_of[3], 1), 0, NXS - 1).astype(jnp.int32),
        "rec_slot": draw_rec_slot(jax.random.fold_in(streams_of[5], 71), 0),
    }


def dft_factors(freq_bins, samples):
    sample_index = jnp.arange(samples, dtype=jnp.int32)
    phase_index = jnp.remainder(sample_index[:, None] * freq_bins[None, :], samples)
    angle_rad = phase_index.astype(jnp.float32) * (2.0 * math.pi / samples)
    factor = 1.0 / math.sqrt(samples)
    return ((jnp.cos(angle_rad) * factor).astype(jnp.bfloat16), (-jnp.sin(angle_rad) * factor).astype(jnp.bfloat16))

def phase_blocks(freq_bins, positions, total_shots):
    ray_offset = jnp.arange(RAY_PARAM_COUNT, dtype=jnp.int32) - RAY_PARAM_COUNT // 2
    period = NT * RDIV
    product = freq_bins[:, None, None, None] * ray_offset[None, None, None, :] * positions[None, :, :, None]
    angle_rad = jnp.remainder(product, period).astype(jnp.float32) * (2.0 * math.pi / period)
    factor = 1.0 / math.sqrt(total_shots)
    cosine = (jnp.cos(angle_rad) * factor).astype(jnp.bfloat16)
    sine_part = (jnp.sin(angle_rad) * factor).astype(jnp.bfloat16)
    upper_half = jnp.concatenate([cosine, -sine_part], axis=3)
    lower_half = jnp.concatenate([sine_part, cosine], axis=3)
    stacked = jnp.stack([upper_half, lower_half], axis=2)
    return stacked.reshape(freq_bins.shape[0], positions.shape[0] * 2 * positions.shape[1], 2 * RAY_PARAM_COUNT)

def row_layout(counts, starts, row_total, shot_total):
    shot_end = jnp.cumsum(counts).astype(jnp.int32)
    row_index = jnp.arange(row_total, dtype=jnp.int32)
    row_shot = lax.optimization_barrier(jnp.sum((row_index[:, None] >= shot_end[None, :]).astype(jnp.int32), axis=1)).astype(jnp.int32)
    begins = (shot_end - counts).astype(jnp.int32)
    onehot = row_shot[:, None] == jnp.arange(shot_total, dtype=jnp.int32)[None, :]
    row_begin = lax.optimization_barrier(jnp.sum(jnp.where(onehot, begins[None, :], 0), axis=1)).astype(jnp.int32)
    row_start = lax.optimization_barrier(jnp.sum(jnp.where(onehot, starts[None, :], 0), axis=1)).astype(jnp.int32)
    receiver = jnp.remainder(row_start + row_index - row_begin, NREC).astype(jnp.int32)
    return (row_shot, receiver)

def reference(traces, trace_counts, aperture_start, shot_position, rec_slot):
    devices = traces.shape[0] // ROW_DEV
    freq_bins = F0 + jnp.arange(FREQUENCY_COUNT, dtype=jnp.int32)
    cosine_table, sine_table = dft_factors(freq_bins, NT)
    transform = jnp.concatenate([cosine_table, sine_table], axis=1).astype(jnp.float32)
    blocks = traces.reshape(devices, ROW_DEV, NT)
    starts = aperture_start.reshape(devices, SHOTS_PER_UNIT)
    positions = shot_position.reshape(devices, SHOTS_PER_UNIT)

    def one_block(running, inputs):
        block_rows, counts, block_starts, block_positions = inputs
        spectra = jnp.dot(block_rows.astype(jnp.float32), transform, precision=lax.Precision.HIGHEST).astype(jnp.bfloat16)
        row_shot, receiver = row_layout(counts, block_starts, ROW_DEV, SHOTS_PER_UNIT)
        row_slot = rec_slot[receiver]
        filled_lattice = jnp.zeros((TOTAL_SLOTS, FREQUENCY_COUNT, 2 * SHOTS_PER_UNIT), jnp.bfloat16)
        filled_lattice = filled_lattice.at[row_slot, :, row_shot].set(spectra[:, :FREQUENCY_COUNT])
        filled_lattice = filled_lattice.at[row_slot, :, SHOTS_PER_UNIT + row_shot].set(spectra[:, FREQUENCY_COUNT:])
        phases = phase_blocks(freq_bins, block_positions[None, :], SHOTS)
        block_term = jnp.einsum('xfs,fsq->xfq', filled_lattice.astype(jnp.float32), phases.astype(jnp.float32), precision=lax.Precision.HIGHEST)
        return (running + block_term, None)
    initial_value = jnp.zeros((TOTAL_SLOTS, FREQUENCY_COUNT, 2 * RAY_PARAM_COUNT), jnp.float32)
    running, unused = lax.scan(one_block, initial_value, (blocks, trace_counts, starts, positions))
    return running.astype(jnp.bfloat16)
```

```python
import math

import jax
import jax.numpy as jnp
import ml_dtypes
import numpy as np
from jax import lax
from jax.experimental import pallas as pl
from jax.experimental.pallas import tpu as pltpu
from jax.sharding import PartitionSpec as P

NT = 2048
FREQUENCY_COUNT = 256
F0 = 8
RAY_PARAM_COUNT = 128
NREC = 512
RDIV = 16
SLAB_SLOTS = 48
ROWS = 3072
UNIT = 8
FREQ_DEV = 8
SLAB_DEV = 16
DEVICES = FREQ_DEV * SLAB_DEV
SLOTS = SLAB_SLOTS * SLAB_DEV
FB = FREQUENCY_COUNT // FREQ_DEV
VALUES = 2 * FREQUENCY_COUNT
SHOTS = UNIT * DEVICES
DFT_ROWS = 512
DFT_STEPS = ROWS // DFT_ROWS
LIMIT = 60 * 2**20


def dft_table():
    column = np.arange(VALUES)
    owner, within = column // (2 * FB), column % (2 * FB)
    bins = F0 + owner * FB + within % FB
    angle = (np.arange(NT)[:, None] * bins[None, :] % NT) * (2.0 * math.pi / NT)
    factor = 1.0 / math.sqrt(NT)
    table = np.where((within // FB == 0)[None, :], np.cos(angle), -np.sin(angle)) * factor
    return table.astype(np.float32).astype(ml_dtypes.bfloat16)


def spread_kernel(counts, starts, traces, table, rec_slot, out, spectra, placed):
    step = pl.program_id(0)

    @pl.when(step == 0)
    def _():
        spectra[ROWS:, :] = jnp.zeros((spectra.shape[0] - ROWS, VALUES), jnp.bfloat16)

    @pl.when(step < DFT_STEPS)
    def _():
        rows = pl.multiple_of(step * DFT_ROWS, DFT_ROWS)
        spectra[pl.ds(rows, DFT_ROWS), :] = jnp.dot(
            traces[...], table[...], preferred_element_type=jnp.float32
        ).astype(jnp.bfloat16)

    @pl.when(step >= DFT_STEPS)
    def _():
        quarter = step - DFT_STEPS
        for half in range(2):
            shot = half * 4 + quarter
            begin = jnp.int32(0)
            for k in range(UNIT):
                begin = begin + jnp.where(k < shot, counts[0, k], 0)
            count = counts[0, shot]
            start = starts[shot]
            base = pl.multiple_of((begin // 16) * 16, 16)
            skip = begin - base
            shift = lax.rem(skip - start + NREC, NREC)
            slots = pltpu.roll(rec_slot[...], shift, 1)[:1]

            def place(depth):
                names = slots if depth <= NREC else jnp.concatenate([slots, slots[:, : depth - NREC]], axis=1)
                names = names[:, :depth]
                lane = lax.broadcasted_iota(jnp.int32, (1, depth), 1) - skip
                names = jnp.where((lane >= 0) & (lane < count), names, -1)
                onehot = (lax.broadcasted_iota(jnp.int32, (SLOTS, depth), 0) == names).astype(jnp.float32)
                placed[half] = jnp.dot(
                    onehot.astype(jnp.bfloat16),
                    spectra[pl.ds(base, depth), :],
                    preferred_element_type=jnp.float32,
                )

            small = skip + count <= NREC

            @pl.when(small)
            def _():
                place(NREC)

            @pl.when(jnp.logical_not(small))
            def _():
                place(NREC + 256)

        low = lax.broadcasted_iota(jnp.int32, (SLOTS, 128), 1) < 64
        for pair in range(FREQ_DEV // 2):
            first = placed[0, :, pair * 128 : pair * 128 + 128]
            second = placed[1, :, pair * 128 : pair * 128 + 128]
            even = jnp.where(low, first, pltpu.roll(second, 64, 1)).astype(jnp.bfloat16)
            odd = jnp.where(low, pltpu.roll(first, 64, 1), second).astype(jnp.bfloat16)
            own = 2 * pair * SLAB_DEV
            out[own : own + SLAB_DEV, 0] = even.reshape(SLAB_DEV, SLAB_SLOTS, 128)
            out[own + SLAB_DEV : own + 2 * SLAB_DEV, 0] = odd.reshape(SLAB_DEV, SLAB_SLOTS, 128)


def spread(traces, counts, starts, rec_slot):
    return pl.pallas_call(
        spread_kernel,
        grid=(DFT_STEPS + 4,),
        in_specs=[
            pl.BlockSpec(memory_space=pltpu.SMEM),
            pl.BlockSpec(memory_space=pltpu.SMEM),
            pl.BlockSpec((DFT_ROWS, NT), lambda i: (jnp.minimum(i, DFT_STEPS - 1), 0)),
            pl.BlockSpec((NT, VALUES), lambda i: (0, 0)),
            pl.BlockSpec((8, NREC), lambda i: (0, 0)),
        ],
        out_specs=pl.BlockSpec(
            (DEVICES, 1, SLAB_SLOTS, 128), lambda i: (0, jnp.maximum(i - DFT_STEPS, 0), 0, 0)
        ),
        out_shape=jax.ShapeDtypeStruct((DEVICES, 4, SLAB_SLOTS, 128), jnp.bfloat16),
        scratch_shapes=[
            pltpu.VMEM((ROWS + 768, VALUES), jnp.bfloat16),
            pltpu.VMEM((2, SLOTS, VALUES), jnp.float32),
        ],
        compiler_params=pltpu.CompilerParams(vmem_limit_bytes=LIMIT),
    )(counts, starts, traces, jnp.asarray(dft_table()), jnp.broadcast_to(rec_slot[None, :], (8, NREC)))


PHASE_ROWS = 128


def phase_kernel(first_bin, positions, out):
    period = NT * RDIV
    unit = 2.0 * math.pi / period
    scale = 1.0 / math.sqrt(SHOTS)
    tile = 16
    ray = lax.broadcasted_iota(jnp.int32, (tile, RAY_PARAM_COUNT), 1) - RAY_PARAM_COUNT // 2

    def turn(k):
        centred = ((k + period // 2) & (period - 1)) - period // 2
        angle = centred.astype(jnp.float32) * unit
        return jnp.cos(angle), jnp.sin(angle)

    def body(t, carry):
        rows = pl.multiple_of(t * tile, tile)
        delay = positions[pl.ds(rows, tile), :] * ray
        step_cos, step_sin = turn(delay)
        c, s = turn(delay * first_bin[0])
        c, s = c * scale, s * scale
        for f in range(FB):
            out[f, pl.ds(rows, tile), :RAY_PARAM_COUNT] = c.astype(jnp.bfloat16)
            out[f, pl.ds(rows, tile), RAY_PARAM_COUNT:] = s.astype(jnp.bfloat16)
            c, s = c * step_cos - s * step_sin, s * step_cos + c * step_sin
        return carry

    lax.fori_loop(0, PHASE_ROWS // tile, body, 0)


def phases(first_bin, positions):
    return pl.pallas_call(
        phase_kernel,
        grid=(SHOTS // PHASE_ROWS,),
        in_specs=[
            pl.BlockSpec(memory_space=pltpu.SMEM),
            pl.BlockSpec((PHASE_ROWS, RAY_PARAM_COUNT), lambda i: (i, 0)),
        ],
        out_specs=pl.BlockSpec((FB, PHASE_ROWS, 2 * RAY_PARAM_COUNT), lambda i: (0, i, 0)),
        out_shape=jax.ShapeDtypeStruct((FB, SHOTS, 2 * RAY_PARAM_COUNT), jnp.bfloat16),
        compiler_params=pltpu.CompilerParams(vmem_limit_bytes=LIMIT),
    )(first_bin, positions)


PART = 16
TURN_STEPS = 4 * (SLAB_SLOTS // PART)
GROUP = 4
LANES = 2 * SLAB_SLOTS


def encode_kernel(blocks, table, out, wide, lattice, encoded):
    step = pl.program_id(0)

    @pl.when(step < TURN_STEPS)
    def _():
        quarter = step // (SLAB_SLOTS // PART)
        part = lax.rem(step, SLAB_SLOTS // PART)
        wide[...] = blocks[...].reshape(DEVICES * PART, 128).astype(jnp.float32)
        eye = (
            lax.broadcasted_iota(jnp.int32, (128, 128), 0) == lax.broadcasted_iota(jnp.int32, (128, 128), 1)
        ).astype(jnp.float32).astype(jnp.bfloat16)
        for s in range(PART):
            rows = wide[pl.ds(s, DEVICES, stride=PART), :].astype(jnp.bfloat16)
            turned = lax.dot_general(
                eye, rows, (((1,), (1,)), ((), ())), preferred_element_type=jnp.float32
            )
            for half in range(2):
                for c in range(2):
                    at = half * 64 + c * FB
                    lattice[
                        half * 4 + quarter, pl.ds(c * SLAB_SLOTS + part * PART + s, FB, stride=LANES), :
                    ] = turned[at : at + FB, :]

    @pl.when(step >= TURN_STEPS)
    def _():
        group = step - TURN_STEPS
        for k in range(GROUP):
            f = group * GROUP + k
            at = pl.multiple_of(f * LANES, LANES)
            rows = jnp.concatenate(
                [lattice[o, pl.ds(at, LANES), :].astype(jnp.bfloat16) for o in range(UNIT)], axis=1
            )
            both = jnp.dot(rows, table[k], preferred_element_type=jnp.float32)
            re, im = both[:SLAB_SLOTS], both[SLAB_SLOTS:]
            n = RAY_PARAM_COUNT
            encoded[0, pl.ds(f, SLAB_SLOTS, stride=FB), :] = re[:, :n] + im[:, n:]
            encoded[1, pl.ds(f, SLAB_SLOTS, stride=FB), :] = im[:, :n] - re[:, n:]

    @pl.when(step == pl.num_programs(0) - 1)
    def _():
        for h in range(2):
            out[:, :, h * RAY_PARAM_COUNT : (h + 1) * RAY_PARAM_COUNT] = (
                encoded[h].reshape(SLAB_SLOTS, FB, RAY_PARAM_COUNT).astype(jnp.bfloat16)
            )


def encode(blocks, table):
    parts = SLAB_SLOTS // PART
    return pl.pallas_call(
        encode_kernel,
        grid=(TURN_STEPS + FB // GROUP,),
        in_specs=[
            pl.BlockSpec(
                (DEVICES, 1, PART, 128),
                lambda i: (0, jnp.minimum(i, TURN_STEPS - 1) // parts, lax.rem(jnp.minimum(i, TURN_STEPS - 1), parts), 0),
            ),
            pl.BlockSpec(
                (GROUP, SHOTS, 2 * RAY_PARAM_COUNT), lambda i: (jnp.maximum(i - TURN_STEPS, 0), 0, 0)
            ),
        ],
        out_specs=pl.BlockSpec((SLAB_SLOTS, FB, 2 * RAY_PARAM_COUNT), lambda i: (0, 0, 0)),
        out_shape=jax.ShapeDtypeStruct((SLAB_SLOTS, FB, 2 * RAY_PARAM_COUNT), jnp.bfloat16),
        scratch_shapes=[
            pltpu.VMEM((DEVICES * PART, 128), jnp.float32),
            pltpu.VMEM((UNIT, FB * LANES, 128), jnp.float32),
            pltpu.VMEM((2, SLAB_SLOTS * FB, RAY_PARAM_COUNT), jnp.float32),
        ],
        compiler_params=pltpu.CompilerParams(vmem_limit_bytes=LIMIT),
    )(blocks, table)


def on_device(traces, trace_counts, aperture_start, shot_position, rec_slot):
    blocks = spread(traces, trace_counts, aperture_start, rec_slot)
    blocks, own_positions = lax.optimization_barrier((blocks, shot_position))
    received = lax.all_to_all(blocks, ("freq", "slab"), split_axis=0, concat_axis=0, tiled=True)
    positions = lax.all_gather(own_positions, ("freq", "slab"), axis=0, tiled=True)
    ordered = positions.reshape(DEVICES, UNIT).T.reshape(SHOTS, 1)
    first_bin = (F0 + lax.axis_index("freq") * FB).astype(jnp.int32).reshape(1)
    table = phases(first_bin, jnp.broadcast_to(ordered, (SHOTS, RAY_PARAM_COUNT)))
    return encode(received, table)


def solution(mesh):
    return jax.shard_map(
        on_device,
        mesh=mesh,
        in_specs=(
            P(("freq", "slab"), None),
            P(("freq", "slab"), None),
            P(("freq", "slab")),
            P(("freq", "slab")),
            P(),
        ),
        out_specs=P("slab", "freq", None),
        check_vma=False,
    )
```

```python
import math

import jax
import jax.numpy as jnp
import ml_dtypes
import numpy as np
from jax import lax
from jax.experimental import pallas as pl
from jax.experimental.pallas import tpu as pltpu
from jax.sharding import PartitionSpec as P

NT = 2048
FREQUENCY_COUNT = 256
F0 = 8
RAY_PARAM_COUNT = 128
NREC = 512
RDIV = 16
SLAB_SLOTS = 48
ROWS = 3072
UNIT = 8
FREQ_DEV = 8
SLAB_DEV = 16
DEVICES = FREQ_DEV * SLAB_DEV
SLOTS = SLAB_SLOTS * SLAB_DEV
FB = FREQUENCY_COUNT // FREQ_DEV
PASSES = 2
FC = FB // PASSES
VALUES = 2 * FC * FREQ_DEV
SPAN = 2 * FC
SIDE = 128 // SPAN
LAYERS = UNIT // SIDE
NOTE_ROWS = 8
SHOTS = UNIT * DEVICES
DFT_ROWS = 512
DFT_STEPS = ROWS // DFT_ROWS
LIMIT = 60 * 2**20


def dft_table(part):
    column = np.arange(VALUES)
    owner, within = column // SPAN, column % SPAN
    bins = F0 + owner * FB + part * FC + within % FC
    angle = (np.arange(NT)[:, None] * bins[None, :] % NT) * (2.0 * math.pi / NT)
    factor = 1.0 / math.sqrt(NT)
    table = np.where((within // FC == 0)[None, :], np.cos(angle), -np.sin(angle)) * factor
    return table.astype(np.float32).astype(ml_dtypes.bfloat16)


def spread_kernel(counts, starts, positions, traces, table, rec_slot, out, spectra, placed):
    step = pl.program_id(0)

    @pl.when(step == 0)
    def _():
        spectra[ROWS:, :] = jnp.zeros((spectra.shape[0] - ROWS, VALUES), jnp.bfloat16)

    @pl.when(step < DFT_STEPS)
    def _():
        rows = pl.multiple_of(step * DFT_ROWS, DFT_ROWS)
        spectra[pl.ds(rows, DFT_ROWS), :] = jnp.dot(
            traces[...], table[...], preferred_element_type=jnp.float32
        ).astype(jnp.bfloat16)

    @pl.when((step >= DFT_STEPS) & (step < DFT_STEPS + LAYERS))
    def _():
        layer = step - DFT_STEPS
        for side in range(SIDE):
            shot = layer * SIDE + side
            begin = jnp.int32(0)
            for k in range(UNIT):
                begin = begin + jnp.where(k < shot, counts[0, k], 0)
            count = counts[0, shot]
            start = starts[shot]
            base = pl.multiple_of((begin // 16) * 16, 16)
            skip = begin - base
            shift = lax.rem(skip - start + NREC, NREC)
            slots = pltpu.roll(rec_slot[...], shift, 1)[:1]

            def place(depth):
                names = slots if depth <= NREC else jnp.concatenate([slots, slots[:, : depth - NREC]], axis=1)
                names = names[:, :depth]
                lane = lax.broadcasted_iota(jnp.int32, (1, depth), 1) - skip
                names = jnp.where((lane >= 0) & (lane < count), names, -1)
                onehot = (lax.broadcasted_iota(jnp.int32, (SLOTS, depth), 0) == names).astype(jnp.float32)
                placed[side] = jnp.dot(
                    onehot.astype(jnp.bfloat16),
                    spectra[pl.ds(base, depth), :],
                    preferred_element_type=jnp.float32,
                )

            small = skip + count <= NREC

            @pl.when(small)
            def _():
                place(NREC)

            @pl.when(jnp.logical_not(small))
            def _():
                place(NREC + 256)

        group = lax.broadcasted_iota(jnp.int32, (SLOTS, 128), 1) // SPAN
        for tile in range(VALUES // 128):
            pieces = [placed[side, :, tile * 128 : tile * 128 + 128] for side in range(SIDE)]
            for k in range(SIDE):
                joined = pieces[k]
                for side in range(SIDE):
                    if side != k:
                        moved = pltpu.roll(pieces[side], (side - k) * SPAN % 128, 1)
                        joined = jnp.where(group == side, moved, joined)
                joined = jnp.where(group == k, pieces[k], joined).astype(jnp.bfloat16)
                owner = tile * SIDE + k
                out[owner * SLAB_DEV : (owner + 1) * SLAB_DEV] = joined.reshape(SLAB_DEV, SLAB_SLOTS, 128)

    @pl.when(step == DFT_STEPS + LAYERS)
    def _():
        lane = lax.broadcasted_iota(jnp.int32, (1, 16, 128), 2)
        note = jnp.zeros((1, 16, 128), jnp.int32)
        for k in range(UNIT):
            x = positions[k]
            note = jnp.where(lane == k, x // 64, note)
            note = jnp.where(lane == UNIT + k, lax.rem(x, 64), note)
        note = note.astype(jnp.float32).astype(jnp.bfloat16)
        out[:, :16] = jnp.broadcast_to(note, (DEVICES, 16, 128))


def spread(part, traces, counts, starts, positions, rec_slot):
    noted = part == 0
    return pl.pallas_call(
        spread_kernel,
        grid=(DFT_STEPS + LAYERS + noted,),
        in_specs=[
            pl.BlockSpec(memory_space=pltpu.SMEM),
            pl.BlockSpec(memory_space=pltpu.SMEM),
            pl.BlockSpec(memory_space=pltpu.SMEM),
            pl.BlockSpec((DFT_ROWS, NT), lambda i: (jnp.minimum(i, DFT_STEPS - 1), 0)),
            pl.BlockSpec((NT, VALUES), lambda i: (0, 0)),
            pl.BlockSpec((8, NREC), lambda i: (0, 0)),
        ],
        out_specs=pl.BlockSpec(
            (DEVICES, SLAB_SLOTS, 128), lambda i: (0, jnp.maximum(i - DFT_STEPS, 0), 0)
        ),
        out_shape=jax.ShapeDtypeStruct(
            (DEVICES, LAYERS * SLAB_SLOTS + NOTE_ROWS * noted, 128), jnp.bfloat16
        ),
        scratch_shapes=[
            pltpu.VMEM((ROWS + 768, VALUES), jnp.bfloat16),
            pltpu.VMEM((SIDE, SLOTS, VALUES), jnp.float32),
        ],
        compiler_params=pltpu.CompilerParams(vmem_limit_bytes=LIMIT),
    )(counts, starts, positions, traces, jnp.asarray(dft_table(part)), jnp.broadcast_to(rec_slot[None, :], (8, NREC)))


PHASE_ROWS = 128


def phase_kernel(first_bin, positions, out):
    period = NT * RDIV
    unit = 2.0 * math.pi / period
    scale = 1.0 / math.sqrt(SHOTS)
    tile = 16
    ray = lax.broadcasted_iota(jnp.int32, (tile, RAY_PARAM_COUNT), 1) - RAY_PARAM_COUNT // 2

    def turn(k):
        centred = ((k + period // 2) & (period - 1)) - period // 2
        angle = centred.astype(jnp.float32) * unit
        return jnp.cos(angle), jnp.sin(angle)

    def body(t, carry):
        rows = pl.multiple_of(t * tile, tile)
        delay = positions[pl.ds(rows, tile), :] * ray
        step_cos, step_sin = turn(delay)
        c, s = turn(delay * first_bin[0])
        c, s = c * scale, s * scale
        for f in range(FB):
            out[f, pl.ds(rows, tile), :RAY_PARAM_COUNT] = c.astype(jnp.bfloat16)
            out[f, pl.ds(rows, tile), RAY_PARAM_COUNT:] = s.astype(jnp.bfloat16)
            c, s = c * step_cos - s * step_sin, s * step_cos + c * step_sin
        return carry

    lax.fori_loop(0, PHASE_ROWS // tile, body, 0)


def phases(first_bin, positions):
    return pl.pallas_call(
        phase_kernel,
        grid=(SHOTS // PHASE_ROWS,),
        in_specs=[
            pl.BlockSpec(memory_space=pltpu.SMEM),
            pl.BlockSpec((PHASE_ROWS, RAY_PARAM_COUNT), lambda i: (i, 0)),
        ],
        out_specs=pl.BlockSpec((FB, PHASE_ROWS, 2 * RAY_PARAM_COUNT), lambda i: (0, i, 0)),
        out_shape=jax.ShapeDtypeStruct((FB, SHOTS, 2 * RAY_PARAM_COUNT), jnp.bfloat16),
        compiler_params=pltpu.CompilerParams(vmem_limit_bytes=LIMIT),
    )(first_bin, positions)


PART = 16
PARTS = SLAB_SLOTS // PART
TURN_STEPS = LAYERS * PARTS
GROUP = 4
LANES = 2 * SLAB_SLOTS


def encode_kernel(blocks, table, out, wide, lattice, encoded):
    step = pl.program_id(0)

    @pl.when(step < TURN_STEPS)
    def _():
        layer = step // PARTS
        part = lax.rem(step, PARTS)
        wide[...] = blocks[...].reshape(DEVICES * PART, 128).astype(jnp.float32)
        eye = (
            lax.broadcasted_iota(jnp.int32, (128, 128), 0) == lax.broadcasted_iota(jnp.int32, (128, 128), 1)
        ).astype(jnp.float32).astype(jnp.bfloat16)
        for s in range(PART):
            rows = wide[pl.ds(s, DEVICES, stride=PART), :].astype(jnp.bfloat16)
            turned = lax.dot_general(
                eye, rows, (((1,), (1,)), ((), ())), preferred_element_type=jnp.float32
            )
            for side in range(SIDE):
                for c in range(2):
                    at = side * SPAN + c * FC
                    lattice[
                        layer * SIDE + side, pl.ds(c * SLAB_SLOTS + part * PART + s, FC, stride=LANES), :
                    ] = turned[at : at + FC, :]

    @pl.when(step >= TURN_STEPS)
    def _():
        group = step - TURN_STEPS
        for k in range(GROUP):
            f = group * GROUP + k
            at = pl.multiple_of(f * LANES, LANES)
            rows = jnp.concatenate(
                [lattice[o, pl.ds(at, LANES), :].astype(jnp.bfloat16) for o in range(UNIT)], axis=1
            )
            both = jnp.dot(rows, table[k], preferred_element_type=jnp.float32)
            re, im = both[:SLAB_SLOTS], both[SLAB_SLOTS:]
            n = RAY_PARAM_COUNT
            encoded[0, pl.ds(f, SLAB_SLOTS, stride=FC), :] = re[:, :n] + im[:, n:]
            encoded[1, pl.ds(f, SLAB_SLOTS, stride=FC), :] = im[:, :n] - re[:, n:]

    @pl.when(step == pl.num_programs(0) - 1)
    def _():
        for h in range(2):
            out[:, :, h * RAY_PARAM_COUNT : (h + 1) * RAY_PARAM_COUNT] = (
                encoded[h].reshape(SLAB_SLOTS, FC, RAY_PARAM_COUNT).astype(jnp.bfloat16)
            )


def encode(part, blocks, table):
    return pl.pallas_call(
        encode_kernel,
        grid=(TURN_STEPS + FC // GROUP,),
        in_specs=[
            pl.BlockSpec((DEVICES, PART, 128), lambda i: (0, jnp.minimum(i, TURN_STEPS - 1), 0)),
            pl.BlockSpec(
                (GROUP, SHOTS, 2 * RAY_PARAM_COUNT),
                lambda i: (part * (FC // GROUP) + jnp.maximum(i - TURN_STEPS, 0), 0, 0),
            ),
        ],
        out_specs=pl.BlockSpec((SLAB_SLOTS, FC, 2 * RAY_PARAM_COUNT), lambda i: (0, 0, 0)),
        out_shape=jax.ShapeDtypeStruct((SLAB_SLOTS, FC, 2 * RAY_PARAM_COUNT), jnp.bfloat16),
        scratch_shapes=[
            pltpu.VMEM((DEVICES * PART, 128), jnp.float32),
            pltpu.VMEM((UNIT, FC * LANES, 128), jnp.float32),
            pltpu.VMEM((2, SLAB_SLOTS * FC, RAY_PARAM_COUNT), jnp.float32),
        ],
        compiler_params=pltpu.CompilerParams(vmem_limit_bytes=LIMIT),
    )(blocks, table)


def on_device(traces, trace_counts, aperture_start, shot_position, rec_slot):
    own = (trace_counts, aperture_start, shot_position, rec_slot)
    everyone = ("freq", "slab")
    first = lax.all_to_all(spread(0, traces, *own), everyone, split_axis=0, concat_axis=0, tiled=True)
    second = lax.all_to_all(spread(1, traces, *own), everyone, split_axis=0, concat_axis=0, tiled=True)
    note = first[:, LAYERS * SLAB_SLOTS, : 2 * UNIT].astype(jnp.int32)
    positions = note[:, :UNIT] * 64 + note[:, UNIT:]
    ordered = positions.T.reshape(SHOTS, 1)
    first_bin = (F0 + lax.axis_index("freq") * FB).astype(jnp.int32).reshape(1)
    table = phases(first_bin, jnp.broadcast_to(ordered, (SHOTS, RAY_PARAM_COUNT)))
    return jnp.concatenate([encode(0, first, table), encode(1, second, table)], axis=1)


def solution(mesh):
    return jax.shard_map(
        on_device,
        mesh=mesh,
        in_specs=(
            P(("freq", "slab"), None),
            P(("freq", "slab"), None),
            P(("freq", "slab")),
            P(("freq", "slab")),
            P(),
        ),
        out_specs=P("slab", "freq", None),
        check_vma=False,
    )
```

```python
import math

import jax
import jax.numpy as jnp
import ml_dtypes
import numpy as np
from jax import lax
from jax.experimental import pallas as pl
from jax.experimental.pallas import tpu as pltpu
from jax.sharding import PartitionSpec as P

NT = 2048
FREQUENCY_COUNT = 256
F0 = 8
RAY_PARAM_COUNT = 128
NREC = 512
RDIV = 16
SLAB_SLOTS = 48
ROWS = 3072
UNIT = 8
FREQ_DEV = 8
SLAB_DEV = 16
DEVICES = FREQ_DEV * SLAB_DEV
SLOTS = SLAB_SLOTS * SLAB_DEV
FB = FREQUENCY_COUNT // FREQ_DEV
PASSES = 2
FC = FB // PASSES
VALUES = 2 * FC * FREQ_DEV
SPAN = 2 * FC
SIDE = 128 // SPAN
LAYERS = UNIT // SIDE
NOTE_ROWS = 8
SHOTS = UNIT * DEVICES
DFT_ROWS = 512
DFT_STEPS = ROWS // DFT_ROWS
LIMIT = 60 * 2**20


def dft_table(part):
    column = np.arange(VALUES)
    owner, within = column // SPAN, column % SPAN
    bins = F0 + owner * FB + part * FC + within % FC
    angle = (np.arange(NT)[:, None] * bins[None, :] % NT) * (2.0 * math.pi / NT)
    factor = 1.0 / math.sqrt(NT)
    table = np.where((within // FC == 0)[None, :], np.cos(angle), -np.sin(angle)) * factor
    return table.astype(np.float32).astype(ml_dtypes.bfloat16)


def spread_kernel(counts, starts, positions, rec_slot, traces, table, out, rows_in, factors, spectra, placed, stage, in_sem, out_sem):
    def rows_copy(i):
        at = pl.ds(pl.multiple_of(i * DFT_ROWS, DFT_ROWS), DFT_ROWS)
        return pltpu.make_async_copy(traces.at[at], rows_in.at[at], in_sem.at[i])

    def owner_copy(owner):
        at = pl.ds(owner * SLAB_DEV, SLAB_DEV)
        return pltpu.make_async_copy(stage.at[at], out.at[at], out_sem.at[owner])

    table_copy = pltpu.make_async_copy(table, factors, in_sem.at[DFT_STEPS])
    table_copy.start()
    for i in range(DFT_STEPS):
        rows_copy(i).start()
    spectra[...] = jnp.zeros(spectra.shape, jnp.bfloat16)
    if stage.shape[1] > LAYERS * SLAB_SLOTS:
        lane = lax.broadcasted_iota(jnp.int32, (1, NOTE_ROWS, 128), 2)
        note = jnp.zeros((1, NOTE_ROWS, 128), jnp.int32)
        for k in range(UNIT):
            x = positions[k]
            note = jnp.where(lane == k, x // 64, note)
            note = jnp.where(lane == UNIT + k, lax.rem(x, 64), note)
        note = note.astype(jnp.float32).astype(jnp.bfloat16)
        stage[:, LAYERS * SLAB_SLOTS :] = jnp.broadcast_to(note, (DEVICES, NOTE_ROWS, 128))
    table_copy.wait()
    group = lax.broadcasted_iota(jnp.int32, (SLOTS, 128), 1) // SPAN

    def join(layer):
        at = pl.ds(pl.multiple_of(layer * SLAB_SLOTS, 16), SLAB_SLOTS)
        for tile in range(VALUES // 128):
            pieces = [placed[side, :, tile * 128 : tile * 128 + 128] for side in range(SIDE)]
            for k in range(SIDE):
                joined = pieces[(SIDE - 1 - k) % SIDE]
                for g in range(SIDE - 1):
                    joined = jnp.where(group == g, pieces[(g - k) % SIDE], joined)
                owner = tile * SIDE + k
                stage[owner * SLAB_DEV : (owner + 1) * SLAB_DEV, at] = joined.astype(jnp.bfloat16).reshape(
                    SLAB_DEV, SLAB_SLOTS, 128
                )

                @pl.when(layer == LAYERS - 1)
                def _():
                    owner_copy(owner).start()

    def place(carry):
        shot, begin = carry
        side = lax.rem(shot, SIDE)
        count = counts[0, shot]
        base = pl.multiple_of((begin // 16) * 16, 16)
        skip = begin - base
        shift = lax.rem(skip - starts[shot] + NREC, NREC)
        slots = pltpu.roll(jnp.broadcast_to(rec_slot[...], (8, NREC)), shift, 1)[:1]

        def product(depth):
            names = slots if depth == NREC else jnp.concatenate([slots, slots[:, : depth - NREC]], axis=1)
            lane = lax.broadcasted_iota(jnp.int32, (1, depth), 1) - skip
            names = jnp.where((lane >= 0) & (lane < count), names, -1)
            onehot = (lax.broadcasted_iota(jnp.int32, (SLOTS, depth), 0) == names).astype(jnp.float32)
            found = jnp.dot(
                onehot.astype(jnp.bfloat16),
                spectra[pl.ds(base, depth), :],
                preferred_element_type=jnp.float32,
            )
            for tile in range(VALUES // 128):
                lanes = slice(tile * 128, tile * 128 + 128)
                placed[side, :, lanes] = pltpu.roll(found[:, lanes], side * SPAN, 1)

        small = skip + count <= NREC

        @pl.when(small)
        def _():
            product(NREC)

        @pl.when(jnp.logical_not(small))
        def _():
            product(NREC + 256)

        @pl.when(side == SIDE - 1)
        def _():
            join(shot // SIDE)

        return shot + 1, begin + count

    def block(i, carry):
        rows_copy(i).wait()
        at = pl.ds(pl.multiple_of(i * DFT_ROWS, DFT_ROWS), DFT_ROWS)
        spectra[at, :] = jnp.dot(
            rows_in[at, :], factors[...], preferred_element_type=jnp.float32
        ).astype(jnp.bfloat16)
        have = (i + 1) * DFT_ROWS

        def ready(carry):
            shot, begin = carry
            return (shot < UNIT) & (begin + counts[0, jnp.minimum(shot, UNIT - 1)] <= have)

        return lax.while_loop(ready, place, carry)

    lax.fori_loop(0, DFT_STEPS, block, (jnp.int32(0), jnp.int32(0)))
    for owner in range(FREQ_DEV):
        owner_copy(owner).wait()


def spread(part, traces, counts, starts, positions, rec_slot):
    height = LAYERS * SLAB_SLOTS + (NOTE_ROWS if part == 0 else 0)
    scalars = pl.BlockSpec(memory_space=pltpu.SMEM)
    anywhere = pl.BlockSpec(memory_space=pl.ANY)
    return pl.pallas_call(
        spread_kernel,
        in_specs=[scalars, scalars, scalars, pl.BlockSpec(memory_space=pltpu.VMEM), anywhere, anywhere],
        out_specs=anywhere,
        out_shape=jax.ShapeDtypeStruct((DEVICES, height, 128), jnp.bfloat16),
        scratch_shapes=[
            pltpu.VMEM((ROWS, NT), jnp.bfloat16),
            pltpu.VMEM((NT, VALUES), jnp.bfloat16),
            pltpu.VMEM((ROWS + 768, VALUES), jnp.bfloat16),
            pltpu.VMEM((SIDE, SLOTS, VALUES), jnp.float32),
            pltpu.VMEM((DEVICES, height, 128), jnp.bfloat16),
            pltpu.SemaphoreType.DMA((DFT_STEPS + 1,)),
            pltpu.SemaphoreType.DMA((FREQ_DEV,)),
        ],
        compiler_params=pltpu.CompilerParams(vmem_limit_bytes=LIMIT),
    )(counts, starts, positions, rec_slot.reshape(1, NREC), traces, jnp.asarray(dft_table(part)))


PHASE_ROWS = 128


def phase_kernel(first_bin, positions, out):
    period = NT * RDIV
    unit = 2.0 * math.pi / period
    scale = 1.0 / math.sqrt(SHOTS)
    tile = 16
    ray = lax.broadcasted_iota(jnp.int32, (tile, RAY_PARAM_COUNT), 1) - RAY_PARAM_COUNT // 2

    def turn(k):
        centred = ((k + period // 2) & (period - 1)) - period // 2
        angle = centred.astype(jnp.float32) * unit
        return jnp.cos(angle), jnp.sin(angle)

    def body(t, carry):
        rows = pl.multiple_of(t * tile, tile)
        delay = positions[pl.ds(rows, tile), :] * ray
        step_cos, step_sin = turn(delay)
        c, s = turn(delay * first_bin[0])
        c, s = c * scale, s * scale
        for f in range(FC):
            out[f, pl.ds(rows, tile), :RAY_PARAM_COUNT] = c.astype(jnp.bfloat16)
            out[f, pl.ds(rows, tile), RAY_PARAM_COUNT:] = s.astype(jnp.bfloat16)
            c, s = c * step_cos - s * step_sin, s * step_cos + c * step_sin
        return carry

    lax.fori_loop(0, PHASE_ROWS // tile, body, 0)


def phases(first_bin, positions):
    return pl.pallas_call(
        phase_kernel,
        grid=(SHOTS // PHASE_ROWS,),
        in_specs=[
            pl.BlockSpec(memory_space=pltpu.SMEM),
            pl.BlockSpec((PHASE_ROWS, RAY_PARAM_COUNT), lambda i: (i, 0)),
        ],
        out_specs=pl.BlockSpec((FC, PHASE_ROWS, 2 * RAY_PARAM_COUNT), lambda i: (0, i, 0)),
        out_shape=jax.ShapeDtypeStruct((FC, SHOTS, 2 * RAY_PARAM_COUNT), jnp.bfloat16),
        compiler_params=pltpu.CompilerParams(vmem_limit_bytes=LIMIT),
    )(first_bin, positions)


PART = 16
PARTS = SLAB_SLOTS // PART
WIDE = PART + 8
LANES = 2 * SLAB_SLOTS
TALL = LANES + 8
DEEP = FC + 8
GROUP = 4


def encode_kernel(blocks, table, earlier, out, raw, factors, wide, lattice, encoded, stage, in_sem, table_sem, out_sem):
    def part_copy(p):
        at = pl.ds(pl.multiple_of(p * PART, PART), PART)
        return pltpu.make_async_copy(blocks.at[:, at], raw.at[:, at], in_sem.at[p])

    def table_copy(g):
        at = pl.ds(g * GROUP, GROUP)
        return pltpu.make_async_copy(table.at[at], factors.at[at], table_sem.at[g])

    for p in range(LAYERS * PARTS):
        part_copy(p).start()
    for g in range(FC // GROUP):
        table_copy(g).start()
    if earlier is not None:
        kept = pltpu.make_async_copy(earlier, out.at[:, :FC], out_sem.at[1])
        kept.start()
    flat = wide.reshape(DEVICES * WIDE, 128)

    def turn(p, carry):
        part_copy(p).wait()
        layer, part = p // PARTS, lax.rem(p, PARTS)
        wide[:, :PART] = raw[:, pl.ds(pl.multiple_of(p * PART, PART), PART)].astype(jnp.float32)
        for s in range(PART):
            turned = jnp.transpose(flat[pl.ds(s, DEVICES, stride=WIDE), :])
            for side in range(SIDE):
                for c in range(2):
                    at = side * SPAN + c * FC
                    lattice[
                        layer * SIDE + side, pl.ds(c * SLAB_SLOTS + part * PART + s, FC, stride=TALL), :
                    ] = turned[at : at + FC, :]
        return carry

    lax.fori_loop(0, LAYERS * PARTS, turn, 0)

    def sum_shots(g, carry):
        table_copy(g).wait()
        for k in range(GROUP):
            f = g * GROUP + k
            at = pl.multiple_of(f * TALL, 8)
            rows = jnp.concatenate(
                [lattice[o, pl.ds(at, LANES), :].astype(jnp.bfloat16) for o in range(UNIT)], axis=1
            )
            both = jnp.dot(rows, factors[f], preferred_element_type=jnp.float32)
            re, im = both[:SLAB_SLOTS], both[SLAB_SLOTS:]
            n = RAY_PARAM_COUNT
            encoded[0, pl.ds(f, SLAB_SLOTS, stride=DEEP), :] = re[:, :n] + im[:, n:]
            encoded[1, pl.ds(f, SLAB_SLOTS, stride=DEEP), :] = im[:, :n] - re[:, n:]
        return carry

    lax.fori_loop(0, FC // GROUP, sum_shots, 0)
    for h in range(2):
        stage[:, :, h * RAY_PARAM_COUNT : (h + 1) * RAY_PARAM_COUNT] = (
            encoded[h].reshape(SLAB_SLOTS, DEEP, RAY_PARAM_COUNT)[:, :FC].astype(jnp.bfloat16)
        )
    target = out if earlier is None else out.at[:, FC:]
    last = pltpu.make_async_copy(stage, target, out_sem.at[0])
    last.start()
    if earlier is not None:
        kept.wait()
    last.wait()


def encode(blocks, table, earlier=None):
    anywhere = pl.BlockSpec(memory_space=pl.ANY)

    def kernel(*refs):
        if earlier is None:
            refs = (*refs[:2], None, *refs[2:])
        encode_kernel(*refs)

    operands = (blocks, table) if earlier is None else (blocks, table, earlier)
    height = FC if earlier is None else FB
    return pl.pallas_call(
        kernel,
        in_specs=[anywhere] * len(operands),
        out_specs=anywhere,
        out_shape=jax.ShapeDtypeStruct((SLAB_SLOTS, height, 2 * RAY_PARAM_COUNT), jnp.bfloat16),
        scratch_shapes=[
            pltpu.VMEM((DEVICES, LAYERS * SLAB_SLOTS, 128), jnp.bfloat16),
            pltpu.VMEM((FC, SHOTS, 2 * RAY_PARAM_COUNT), jnp.bfloat16),
            pltpu.VMEM((DEVICES, WIDE, 128), jnp.float32),
            pltpu.VMEM((UNIT, FC * TALL, 128), jnp.float32),
            pltpu.VMEM((2, SLAB_SLOTS * DEEP, RAY_PARAM_COUNT), jnp.float32),
            pltpu.VMEM((SLAB_SLOTS, FC, 2 * RAY_PARAM_COUNT), jnp.bfloat16),
            pltpu.SemaphoreType.DMA((LAYERS * PARTS,)),
            pltpu.SemaphoreType.DMA((FC // GROUP,)),
            pltpu.SemaphoreType.DMA((2,)),
        ],
        compiler_params=pltpu.CompilerParams(vmem_limit_bytes=LIMIT),
    )(*operands)


def on_device(traces, trace_counts, aperture_start, shot_position, rec_slot):
    own = (trace_counts, aperture_start, shot_position, rec_slot)
    everyone = ("freq", "slab")
    first = lax.all_to_all(spread(0, traces, *own), everyone, split_axis=0, concat_axis=0, tiled=True)
    second = lax.all_to_all(spread(1, traces, *own), everyone, split_axis=0, concat_axis=0, tiled=True)
    note = first[:, LAYERS * SLAB_SLOTS, : 2 * UNIT].astype(jnp.int32)
    positions = (note[:, :UNIT] * 64 + note[:, UNIT:]).T.reshape(LAYERS, SIDE, DEVICES)
    turn = lax.rem(SIDE - lax.rem(lax.axis_index("freq"), SIDE), SIDE)
    positions = lax.dynamic_slice_in_dim(jnp.concatenate([positions, positions], axis=1), turn, SIDE, axis=1)
    positions = jnp.broadcast_to(positions.reshape(SHOTS, 1), (SHOTS, RAY_PARAM_COUNT))
    first_bin = (F0 + lax.axis_index("freq") * FB).astype(jnp.int32).reshape(1)
    low = encode(first, phases(first_bin, positions))
    return encode(second, phases(first_bin + FC, positions), low)


def solution(mesh):
    return jax.shard_map(
        on_device,
        mesh=mesh,
        in_specs=(
            P(("freq", "slab"), None),
            P(("freq", "slab"), None),
            P(("freq", "slab")),
            P(("freq", "slab")),
            P(),
        ),
        out_specs=P("slab", "freq", None),
        check_vma=False,
    )
```

```python
import math

import jax
import jax.numpy as jnp
import ml_dtypes
import numpy as np
from jax import lax
from jax.experimental import pallas as pl
from jax.experimental.pallas import tpu as pltpu
from jax.sharding import PartitionSpec as P

NT = 2048
FREQUENCY_COUNT = 256
F0 = 8
RAY_PARAM_COUNT = 128
NREC = 512
RDIV = 16
SLAB_SLOTS = 48
ROWS = 3072
UNIT = 8
FREQ_DEV = 8
SLAB_DEV = 16
DEVICES = FREQ_DEV * SLAB_DEV
SLOTS = SLAB_SLOTS * SLAB_DEV
FB = FREQUENCY_COUNT // FREQ_DEV
PASSES = 2
FC = FB // PASSES
VALUES = 2 * FC * FREQ_DEV
SPAN = 2 * FC
SIDE = 128 // SPAN
LAYERS = UNIT // SIDE
NOTE_ROWS = 8
SHOTS = UNIT * DEVICES
DFT_ROWS = 512
WINDOW = NREC + 256
DFT_STEPS = ROWS // DFT_ROWS
AHEAD = 3
LIMIT = 60 * 2**20


def dft_table(part):
    column = np.arange(VALUES)
    owner, within = column // SPAN, column % SPAN
    bins = F0 + owner * FB + part * FC + within % FC
    angle = (np.arange(NT)[:, None] * bins[None, :] % NT) * (2.0 * math.pi / NT)
    factor = 1.0 / math.sqrt(NT)
    table = np.where((within // FC == 0)[None, :], np.cos(angle), -np.sin(angle)) * factor
    return table.astype(np.float32).astype(ml_dtypes.bfloat16)


def spread_kernel(counts, starts, positions, rec_slot, traces, table, out, rows_in, factors, names, spectra, placed, stage, in_sem, out_sem):
    def rows_copy(i):
        at = pl.ds(pl.multiple_of(i * DFT_ROWS, DFT_ROWS), DFT_ROWS)
        return pltpu.make_async_copy(traces.at[at], rows_in.at[at], in_sem.at[i])

    def owner_copy(owner):
        at = pl.ds(owner * SLAB_DEV, SLAB_DEV)
        return pltpu.make_async_copy(stage.at[at], out.at[at], out_sem.at[owner])

    table_copy = pltpu.make_async_copy(table, factors, in_sem.at[DFT_STEPS])
    table_copy.start()
    for i in range(AHEAD):
        rows_copy(i).start()
    spectra[...] = jnp.zeros(spectra.shape, jnp.bfloat16)
    if stage.shape[1] > LAYERS * SLAB_SLOTS:
        lane = lax.broadcasted_iota(jnp.int32, (1, NOTE_ROWS, 128), 2)
        note = jnp.zeros((1, NOTE_ROWS, 128), jnp.int32)
        for k in range(UNIT):
            x = positions[k]
            note = jnp.where(lane == k, x // 64, note)
            note = jnp.where(lane == UNIT + k, lax.rem(x, 64), note)
        note = note.astype(jnp.float32).astype(jnp.bfloat16)
        stage[:, LAYERS * SLAB_SLOTS :] = jnp.broadcast_to(note, (DEVICES, NOTE_ROWS, 128))
    begin = jnp.int32(0)
    lane = lax.broadcasted_iota(jnp.int32, (1, WINDOW), 1)
    for k in range(UNIT):
        skip = lax.rem(begin, 16)
        shift = lax.rem(skip - starts[k] + NREC, NREC)
        slots = pltpu.roll(jnp.broadcast_to(rec_slot[...], (8, NREC)), shift, 1)[:1]
        slots = jnp.concatenate([slots, slots[:, : WINDOW - NREC]], axis=1)
        names[k : k + 1, :] = jnp.where((lane >= skip) & (lane < skip + counts[0, k]), slots, -1)
        begin = begin + counts[0, k]
    table_copy.wait()
    group = lax.broadcasted_iota(jnp.int32, (SLOTS, 128), 1) // SPAN

    def join(layer):
        at = pl.ds(pl.multiple_of(layer * SLAB_SLOTS, 16), SLAB_SLOTS)
        for tile in range(VALUES // 128):
            pieces = [placed[side, :, tile * 128 : tile * 128 + 128] for side in range(SIDE)]
            for k in range(SIDE):
                joined = pieces[(SIDE - 1 - k) % SIDE]
                for g in range(SIDE - 1):
                    joined = jnp.where(group == g, pieces[(g - k) % SIDE], joined)
                owner = tile * SIDE + k
                stage[owner * SLAB_DEV : (owner + 1) * SLAB_DEV, at] = joined.astype(jnp.bfloat16).reshape(
                    SLAB_DEV, SLAB_SLOTS, 128
                )

                @pl.when(layer == LAYERS - 1)
                def _():
                    owner_copy(owner).start()

    def place(carry):
        shot, begin = carry
        side = lax.rem(shot, SIDE)
        count = counts[0, shot]
        base = pl.multiple_of((begin // 16) * 16, 16)
        skip = begin - base

        def product(depth):
            name = names[pl.ds(shot, 1), :depth]
            onehot = (lax.broadcasted_iota(jnp.int32, (SLOTS, depth), 0) == name).astype(jnp.float32)
            found = jnp.dot(
                onehot.astype(jnp.bfloat16),
                spectra[pl.ds(base, depth), :],
                preferred_element_type=jnp.float32,
            )
            for tile in range(VALUES // 128):
                lanes = slice(tile * 128, tile * 128 + 128)
                placed[side, :, lanes] = pltpu.roll(found[:, lanes], side * SPAN, 1)

        small = skip + count <= NREC

        @pl.when(small)
        def _():
            product(NREC)

        @pl.when(jnp.logical_not(small))
        def _():
            product(WINDOW)

        @pl.when(side == SIDE - 1)
        def _():
            join(shot // SIDE)

        return shot + 1, begin + count

    def block(i, carry):
        rows_copy(i).wait()

        @pl.when(i + AHEAD < DFT_STEPS)
        def _():
            rows_copy(i + AHEAD).start()

        at = pl.ds(pl.multiple_of(i * DFT_ROWS, DFT_ROWS), DFT_ROWS)
        spectra[at, :] = jnp.dot(
            rows_in[at, :], factors[...], preferred_element_type=jnp.float32
        ).astype(jnp.bfloat16)
        have = (i + 1) * DFT_ROWS

        def ready(carry):
            shot, begin = carry
            return (shot < UNIT) & (begin + counts[0, jnp.minimum(shot, UNIT - 1)] <= have)

        return lax.while_loop(ready, place, carry)

    lax.fori_loop(0, DFT_STEPS, block, (jnp.int32(0), jnp.int32(0)))
    for owner in range(FREQ_DEV):
        owner_copy(owner).wait()


def spread(part, traces, counts, starts, positions, rec_slot):
    height = LAYERS * SLAB_SLOTS + (NOTE_ROWS if part == 0 else 0)
    scalars = pl.BlockSpec(memory_space=pltpu.SMEM)
    anywhere = pl.BlockSpec(memory_space=pl.ANY)
    return pl.pallas_call(
        spread_kernel,
        in_specs=[scalars, scalars, scalars, pl.BlockSpec(memory_space=pltpu.VMEM), anywhere, anywhere],
        out_specs=anywhere,
        out_shape=jax.ShapeDtypeStruct((DEVICES, height, 128), jnp.bfloat16),
        scratch_shapes=[
            pltpu.VMEM((ROWS, NT), jnp.bfloat16),
            pltpu.VMEM((NT, VALUES), jnp.bfloat16),
            pltpu.VMEM((UNIT, WINDOW), jnp.int32),
            pltpu.VMEM((ROWS + WINDOW, VALUES), jnp.bfloat16),
            pltpu.VMEM((SIDE, SLOTS, VALUES), jnp.float32),
            pltpu.VMEM((DEVICES, height, 128), jnp.bfloat16),
            pltpu.SemaphoreType.DMA((DFT_STEPS + 1,)),
            pltpu.SemaphoreType.DMA((FREQ_DEV,)),
        ],
        compiler_params=pltpu.CompilerParams(vmem_limit_bytes=LIMIT),
    )(counts, starts, positions, rec_slot.reshape(1, NREC), traces, jnp.asarray(dft_table(part)))


PHASE_ROWS = 128


def phase_kernel(first_bin, positions, out):
    period = NT * RDIV
    unit = 2.0 * math.pi / period
    scale = 1.0 / math.sqrt(SHOTS)
    tile = 16
    ray = lax.broadcasted_iota(jnp.int32, (tile, RAY_PARAM_COUNT), 1) - RAY_PARAM_COUNT // 2

    def turn(k):
        centred = ((k + period // 2) & (period - 1)) - period // 2
        angle = centred.astype(jnp.float32) * unit
        return jnp.cos(angle), jnp.sin(angle)

    def body(t, carry):
        rows = pl.multiple_of(t * tile, tile)
        delay = positions[pl.ds(rows, tile), :] * ray
        step_cos, step_sin = turn(delay)
        c, s = turn(delay * first_bin[0])
        c, s = c * scale, s * scale
        for f in range(FC):
            out[f, pl.ds(rows, tile), :RAY_PARAM_COUNT] = c.astype(jnp.bfloat16)
            out[f, pl.ds(rows, tile), RAY_PARAM_COUNT:] = s.astype(jnp.bfloat16)
            c, s = c * step_cos - s * step_sin, s * step_cos + c * step_sin
        return carry

    lax.fori_loop(0, PHASE_ROWS // tile, body, 0)


def phases(first_bin, positions):
    return pl.pallas_call(
        phase_kernel,
        grid=(SHOTS // PHASE_ROWS,),
        in_specs=[
            pl.BlockSpec(memory_space=pltpu.SMEM),
            pl.BlockSpec((PHASE_ROWS, RAY_PARAM_COUNT), lambda i: (i, 0)),
        ],
        out_specs=pl.BlockSpec((FC, PHASE_ROWS, 2 * RAY_PARAM_COUNT), lambda i: (0, i, 0)),
        out_shape=jax.ShapeDtypeStruct((FC, SHOTS, 2 * RAY_PARAM_COUNT), jnp.bfloat16),
        compiler_params=pltpu.CompilerParams(vmem_limit_bytes=LIMIT),
    )(first_bin, positions)


PART = 16
PARTS = SLAB_SLOTS // PART
WIDE = PART + 8
LANES = 2 * SLAB_SLOTS
TALL = LANES + 8
DEEP = FC + 8
GROUP = 4


def encode_kernel(blocks, table, earlier, out, raw, factors, wide, lattice, encoded, stage, in_sem, table_sem, out_sem):
    def part_copy(p):
        at = pl.ds(pl.multiple_of(p * PART, PART), PART)
        return pltpu.make_async_copy(blocks.at[:, at], raw.at[:, at], in_sem.at[p])

    def table_copy(g):
        at = pl.ds(g * GROUP, GROUP)
        return pltpu.make_async_copy(table.at[at], factors.at[at], table_sem.at[g])

    for p in range(LAYERS * PARTS):
        part_copy(p).start()
    for g in range(FC // GROUP):
        table_copy(g).start()
    if earlier is not None:
        kept = pltpu.make_async_copy(earlier, stage.at[:, :FC], out_sem.at[1])
        kept.start()
    flat = wide.reshape(DEVICES * WIDE, 128)

    def turn(p, carry):
        part_copy(p).wait()
        layer, part = p // PARTS, lax.rem(p, PARTS)
        wide[:, :PART] = raw[:, pl.ds(pl.multiple_of(p * PART, PART), PART)].astype(jnp.float32)
        for s in range(PART):
            turned = jnp.transpose(flat[pl.ds(s, DEVICES, stride=WIDE), :])
            for side in range(SIDE):
                for c in range(2):
                    at = side * SPAN + c * FC
                    lattice[
                        layer * SIDE + side, pl.ds(c * SLAB_SLOTS + part * PART + s, FC, stride=TALL), :
                    ] = turned[at : at + FC, :]
        return carry

    lax.fori_loop(0, LAYERS * PARTS, turn, 0)

    def sum_shots(g, carry):
        table_copy(g).wait()
        for k in range(GROUP):
            f = g * GROUP + k
            at = pl.multiple_of(f * TALL, 8)
            rows = jnp.concatenate(
                [lattice[o, pl.ds(at, LANES), :].astype(jnp.bfloat16) for o in range(UNIT)], axis=1
            )
            both = jnp.dot(rows, factors[f], preferred_element_type=jnp.float32)
            re, im = both[:SLAB_SLOTS], both[SLAB_SLOTS:]
            n = RAY_PARAM_COUNT
            encoded[0, pl.ds(f, SLAB_SLOTS, stride=DEEP), :] = re[:, :n] + im[:, n:]
            encoded[1, pl.ds(f, SLAB_SLOTS, stride=DEEP), :] = im[:, :n] - re[:, n:]
        return carry

    lax.fori_loop(0, FC // GROUP, sum_shots, 0)
    own = slice(0, FC) if earlier is None else slice(FC, FB)
    for h in range(2):
        stage[:, own, h * RAY_PARAM_COUNT : (h + 1) * RAY_PARAM_COUNT] = (
            encoded[h].reshape(SLAB_SLOTS, DEEP, RAY_PARAM_COUNT)[:, :FC].astype(jnp.bfloat16)
        )
    if earlier is not None:
        kept.wait()
    last = pltpu.make_async_copy(stage, out, out_sem.at[0])
    last.start()
    last.wait()


def encode(blocks, table, earlier=None):
    anywhere = pl.BlockSpec(memory_space=pl.ANY)

    def kernel(*refs):
        if earlier is None:
            refs = (*refs[:2], None, *refs[2:])
        encode_kernel(*refs)

    operands = (blocks, table) if earlier is None else (blocks, table, earlier)
    height = FC if earlier is None else FB
    return pl.pallas_call(
        kernel,
        in_specs=[anywhere] * len(operands),
        out_specs=anywhere,
        out_shape=jax.ShapeDtypeStruct((SLAB_SLOTS, height, 2 * RAY_PARAM_COUNT), jnp.bfloat16),
        scratch_shapes=[
            pltpu.VMEM((DEVICES, LAYERS * SLAB_SLOTS, 128), jnp.bfloat16),
            pltpu.VMEM((FC, SHOTS, 2 * RAY_PARAM_COUNT), jnp.bfloat16),
            pltpu.VMEM((DEVICES, WIDE, 128), jnp.float32),
            pltpu.VMEM((UNIT, FC * TALL, 128), jnp.float32),
            pltpu.VMEM((2, SLAB_SLOTS * DEEP, RAY_PARAM_COUNT), jnp.float32),
            pltpu.VMEM((SLAB_SLOTS, height, 2 * RAY_PARAM_COUNT), jnp.bfloat16),
            pltpu.SemaphoreType.DMA((LAYERS * PARTS,)),
            pltpu.SemaphoreType.DMA((FC // GROUP,)),
            pltpu.SemaphoreType.DMA((2,)),
        ],
        compiler_params=pltpu.CompilerParams(vmem_limit_bytes=LIMIT),
    )(*operands)


def on_device(traces, trace_counts, aperture_start, shot_position, rec_slot):
    own = (trace_counts, aperture_start, shot_position, rec_slot)
    everyone = ("freq", "slab")
    first = lax.all_to_all(spread(0, traces, *own), everyone, split_axis=0, concat_axis=0, tiled=True)
    second = lax.all_to_all(spread(1, traces, *own), everyone, split_axis=0, concat_axis=0, tiled=True)
    note = first[:, LAYERS * SLAB_SLOTS, : 2 * UNIT].astype(jnp.int32)
    positions = (note[:, :UNIT] * 64 + note[:, UNIT:]).T.reshape(LAYERS, SIDE, DEVICES)
    turn = lax.rem(SIDE - lax.rem(lax.axis_index("freq"), SIDE), SIDE)
    positions = lax.dynamic_slice_in_dim(jnp.concatenate([positions, positions], axis=1), turn, SIDE, axis=1)
    positions = jnp.broadcast_to(positions.reshape(SHOTS, 1), (SHOTS, RAY_PARAM_COUNT))
    first_bin = (F0 + lax.axis_index("freq") * FB).astype(jnp.int32).reshape(1)
    low = encode(first, phases(first_bin, positions))
    return encode(second, phases(first_bin + FC, positions), low)


def solution(mesh):
    return jax.shard_map(
        on_device,
        mesh=mesh,
        in_specs=(
            P(("freq", "slab"), None),
            P(("freq", "slab"), None),
            P(("freq", "slab")),
            P(("freq", "slab")),
            P(),
        ),
        out_specs=P("slab", "freq", None),
        check_vma=False,
    )
```

```python
import math

import jax
import jax.numpy as jnp
import ml_dtypes
import numpy as np
from jax import lax
from jax.experimental import pallas as pl
from jax.experimental.pallas import tpu as pltpu
from jax.sharding import PartitionSpec as P

NT = 2048
FREQUENCY_COUNT = 256
F0 = 8
RAY_PARAM_COUNT = 128
NREC = 512
RDIV = 16
SLAB_SLOTS = 48
ROWS = 3072
UNIT = 8
FREQ_DEV = 8
SLAB_DEV = 16
DEVICES = FREQ_DEV * SLAB_DEV
SLOTS = SLAB_SLOTS * SLAB_DEV
FB = FREQUENCY_COUNT // FREQ_DEV
PASSES = 2
FC = FB // PASSES
VALUES = 2 * FC * FREQ_DEV
SPAN = 2 * FC
SIDE = 128 // SPAN
LAYERS = UNIT // SIDE
PAIRS = LAYERS * SLAB_SLOTS // 2
NOTE_ROWS = 2
SHOTS = UNIT * DEVICES
DFT_ROWS = 512
WINDOW = NREC + 256
DFT_STEPS = ROWS // DFT_ROWS
AHEAD = 3
LIMIT = 60 * 2**20


def dft_table(part):
    column = np.arange(VALUES)
    owner, within = column // SPAN, column % SPAN
    bins = F0 + owner * FB + part * FC + within % FC
    angle = (np.arange(NT)[:, None] * bins[None, :] % NT) * (2.0 * math.pi / NT)
    factor = 1.0 / math.sqrt(NT)
    table = np.where((within // FC == 0)[None, :], np.cos(angle), -np.sin(angle)) * factor
    return table.astype(np.float32).astype(ml_dtypes.bfloat16)


def spread_kernel(counts, starts, positions, rec_slot, traces, table, out, rows_in, factors, names, spectra, placed, stage, in_sem, out_sem):
    noted = len(stage.shape) == 4

    def rows_copy(i):
        at = pl.ds(pl.multiple_of(i * DFT_ROWS, DFT_ROWS), DFT_ROWS)
        return pltpu.make_async_copy(traces.at[at], rows_in.at[at], in_sem.at[i])

    def owner_copy(owner):
        at = pl.ds(owner * SLAB_DEV, SLAB_DEV)
        return pltpu.make_async_copy(stage.at[at], out.at[at], out_sem.at[owner])

    table_copy = pltpu.make_async_copy(table, factors, in_sem.at[DFT_STEPS])
    table_copy.start()
    for i in range(AHEAD):
        rows_copy(i).start()
    spectra[...] = jnp.zeros(spectra.shape, jnp.bfloat16)
    if noted:
        lane = lax.broadcasted_iota(jnp.int32, (1, 1, NOTE_ROWS, 128), 3)
        note = jnp.zeros((1, 1, NOTE_ROWS, 128), jnp.int32)
        for k in range(UNIT):
            x = positions[k]
            note = jnp.where(lane == k, x // 64, note)
            note = jnp.where(lane == UNIT + k, lax.rem(x, 64), note)
        note = note.astype(jnp.float32).astype(jnp.bfloat16)
        stage[:, PAIRS:] = jnp.broadcast_to(note, (DEVICES, 1, NOTE_ROWS, 128))
    begin = jnp.int32(0)
    lane = lax.broadcasted_iota(jnp.int32, (1, WINDOW), 1)
    for k in range(UNIT):
        skip = lax.rem(begin, 16)
        shift = lax.rem(skip - starts[k] + NREC, NREC)
        slots = pltpu.roll(jnp.broadcast_to(rec_slot[...], (8, NREC)), shift, 1)[:1]
        slots = jnp.concatenate([slots, slots[:, : WINDOW - NREC]], axis=1)
        names[k : k + 1, :] = jnp.where((lane >= skip) & (lane < skip + counts[0, k]), slots, -1)
        begin = begin + counts[0, k]
    table_copy.wait()
    group = lax.broadcasted_iota(jnp.int32, (SLOTS, 128), 1) // SPAN

    def join(layer):
        height = (SLAB_SLOTS // 2, 2) if noted else (SLAB_SLOTS,)
        at = pl.ds(layer * height[0] if noted else pl.multiple_of(layer * SLAB_SLOTS, 16), height[0])
        for tile in range(VALUES // 128):
            pieces = [placed[side, :, tile * 128 : tile * 128 + 128] for side in range(SIDE)]
            for k in range(SIDE):
                joined = pieces[(SIDE - 1 - k) % SIDE]
                for g in range(SIDE - 1):
                    joined = jnp.where(group == g, pieces[(g - k) % SIDE], joined)
                owner = tile * SIDE + k
                stage[owner * SLAB_DEV : (owner + 1) * SLAB_DEV, at] = joined.astype(jnp.bfloat16).reshape(
                    SLAB_DEV, *height, 128
                )

                @pl.when(layer == LAYERS - 1)
                def _():
                    owner_copy(owner).start()

    def place(carry):
        shot, begin = carry
        side = lax.rem(shot, SIDE)
        count = counts[0, shot]
        base = pl.multiple_of((begin // 16) * 16, 16)
        skip = begin - base

        def product(depth):
            name = names[pl.ds(shot, 1), :depth]
            onehot = (lax.broadcasted_iota(jnp.int32, (SLOTS, depth), 0) == name).astype(jnp.float32)
            found = jnp.dot(
                onehot.astype(jnp.bfloat16),
                spectra[pl.ds(base, depth), :],
                preferred_element_type=jnp.float32,
            )
            for tile in range(VALUES // 128):
                lanes = slice(tile * 128, tile * 128 + 128)
                placed[side, :, lanes] = pltpu.roll(found[:, lanes], side * SPAN, 1)

        small = skip + count <= NREC

        @pl.when(small)
        def _():
            product(NREC)

        @pl.when(jnp.logical_not(small))
        def _():
            product(WINDOW)

        @pl.when(side == SIDE - 1)
        def _():
            join(shot // SIDE)

        return shot + 1, begin + count

    def block(i, carry):
        rows_copy(i).wait()

        @pl.when(i + AHEAD < DFT_STEPS)
        def _():
            rows_copy(i + AHEAD).start()

        at = pl.ds(pl.multiple_of(i * DFT_ROWS, DFT_ROWS), DFT_ROWS)
        spectra[at, :] = jnp.dot(
            rows_in[at, :], factors[...], preferred_element_type=jnp.float32
        ).astype(jnp.bfloat16)
        have = (i + 1) * DFT_ROWS

        def ready(carry):
            shot, begin = carry
            return (shot < UNIT) & (begin + counts[0, jnp.minimum(shot, UNIT - 1)] <= have)

        return lax.while_loop(ready, place, carry)

    lax.fori_loop(0, DFT_STEPS, block, (jnp.int32(0), jnp.int32(0)))
    for owner in range(FREQ_DEV):
        owner_copy(owner).wait()


def spread(part, traces, counts, starts, positions, rec_slot):
    rows = (PAIRS + 1, 2) if part == 0 else (LAYERS * SLAB_SLOTS,)
    scalars = pl.BlockSpec(memory_space=pltpu.SMEM)
    anywhere = pl.BlockSpec(memory_space=pl.ANY)
    return pl.pallas_call(
        spread_kernel,
        in_specs=[scalars, scalars, scalars, pl.BlockSpec(memory_space=pltpu.VMEM), anywhere, anywhere],
        out_specs=anywhere,
        out_shape=jax.ShapeDtypeStruct((DEVICES, *rows, 128), jnp.bfloat16),
        scratch_shapes=[
            pltpu.VMEM((ROWS, NT), jnp.bfloat16),
            pltpu.VMEM((NT, VALUES), jnp.bfloat16),
            pltpu.VMEM((UNIT, WINDOW), jnp.int32),
            pltpu.VMEM((ROWS + WINDOW, VALUES), jnp.bfloat16),
            pltpu.VMEM((SIDE, SLOTS, VALUES), jnp.float32),
            pltpu.VMEM((DEVICES, *rows, 128), jnp.bfloat16),
            pltpu.SemaphoreType.DMA((DFT_STEPS + 1,)),
            pltpu.SemaphoreType.DMA((FREQ_DEV,)),
        ],
        compiler_params=pltpu.CompilerParams(vmem_limit_bytes=LIMIT),
    )(counts, starts, positions, rec_slot.reshape(1, NREC), traces, jnp.asarray(dft_table(part)))


PHASE_ROWS = 128


def phase_kernel(first_bin, positions, out):
    period = NT * RDIV
    unit = 2.0 * math.pi / period
    scale = 1.0 / math.sqrt(SHOTS)
    tile = 16
    ray = lax.broadcasted_iota(jnp.int32, (tile, RAY_PARAM_COUNT), 1) - RAY_PARAM_COUNT // 2

    def turn(k):
        centred = ((k + period // 2) & (period - 1)) - period // 2
        angle = centred.astype(jnp.float32) * unit
        return jnp.cos(angle), jnp.sin(angle)

    def body(t, carry):
        rows = pl.multiple_of(t * tile, tile)
        delay = positions[pl.ds(rows, tile), :] * ray
        step_cos, step_sin = turn(delay)
        c, s = turn(delay * first_bin[0])
        c, s = c * scale, s * scale
        for f in range(FC):
            out[f, pl.ds(rows, tile), :RAY_PARAM_COUNT] = c.astype(jnp.bfloat16)
            out[f, pl.ds(rows, tile), RAY_PARAM_COUNT:] = s.astype(jnp.bfloat16)
            c, s = c * step_cos - s * step_sin, s * step_cos + c * step_sin
        return carry

    lax.fori_loop(0, PHASE_ROWS // tile, body, 0)


def phases(first_bin, positions):
    return pl.pallas_call(
        phase_kernel,
        grid=(SHOTS // PHASE_ROWS,),
        in_specs=[
            pl.BlockSpec(memory_space=pltpu.SMEM),
            pl.BlockSpec((PHASE_ROWS, RAY_PARAM_COUNT), lambda i: (i, 0)),
        ],
        out_specs=pl.BlockSpec((FC, PHASE_ROWS, 2 * RAY_PARAM_COUNT), lambda i: (0, i, 0)),
        out_shape=jax.ShapeDtypeStruct((FC, SHOTS, 2 * RAY_PARAM_COUNT), jnp.bfloat16),
        compiler_params=pltpu.CompilerParams(vmem_limit_bytes=LIMIT),
    )(first_bin, positions)


PART = 16
PARTS = SLAB_SLOTS // PART
WIDE = PART + 8
LANES = 2 * SLAB_SLOTS
TALL = LANES + 8
DEEP = FC + 8
GROUP = 4


def encode_kernel(blocks, table, earlier, out, raw, factors, wide, lattice, encoded, stage, in_sem, table_sem, out_sem):
    def part_rows(p):
        if len(raw.shape) == 4:
            return pl.ds(p * (PART // 2), PART // 2)
        return pl.ds(pl.multiple_of(p * PART, PART), PART)

    def part_copy(p):
        at = part_rows(p)
        return pltpu.make_async_copy(blocks.at[:, at], raw.at[:, at], in_sem.at[p])

    def table_copy(g):
        at = pl.ds(g * GROUP, GROUP)
        return pltpu.make_async_copy(table.at[at], factors.at[at], table_sem.at[g])

    for p in range(LAYERS * PARTS):
        part_copy(p).start()
    if earlier is not None:
        kept = pltpu.make_async_copy(earlier, stage.at[:, :FC], out_sem.at[1])
        kept.start()
    flat = wide.reshape(DEVICES * WIDE, 128)

    def turn(p, carry):
        part_copy(p).wait()

        @pl.when(p == 0)
        def _():
            for g in range(FC // GROUP):
                table_copy(g).start()

        layer, part = p // PARTS, lax.rem(p, PARTS)
        wide[:, :PART] = raw[:, part_rows(p)].reshape(DEVICES, PART, 128).astype(jnp.float32)
        for s in range(PART):
            turned = jnp.transpose(flat[pl.ds(s, DEVICES, stride=WIDE), :])
            for side in range(SIDE):
                for c in range(2):
                    at = side * SPAN + c * FC
                    lattice[
                        layer * SIDE + side, pl.ds(c * SLAB_SLOTS + part * PART + s, FC, stride=TALL), :
                    ] = turned[at : at + FC, :]
        return carry

    lax.fori_loop(0, LAYERS * PARTS, turn, 0)

    def sum_shots(g, carry):
        table_copy(g).wait()
        for k in range(GROUP):
            f = g * GROUP + k
            at = pl.multiple_of(f * TALL, 8)
            rows = jnp.concatenate(
                [lattice[o, pl.ds(at, LANES), :].astype(jnp.bfloat16) for o in range(UNIT)], axis=1
            )
            both = jnp.dot(rows, factors[f], preferred_element_type=jnp.float32)
            re, im = both[:SLAB_SLOTS], both[SLAB_SLOTS:]
            n = RAY_PARAM_COUNT
            encoded[0, pl.ds(f, SLAB_SLOTS, stride=DEEP), :] = re[:, :n] + im[:, n:]
            encoded[1, pl.ds(f, SLAB_SLOTS, stride=DEEP), :] = im[:, :n] - re[:, n:]
        return carry

    lax.fori_loop(0, FC // GROUP, sum_shots, 0)
    own = slice(0, FC) if earlier is None else slice(FC, FB)
    for h in range(2):
        stage[:, own, h * RAY_PARAM_COUNT : (h + 1) * RAY_PARAM_COUNT] = (
            encoded[h].reshape(SLAB_SLOTS, DEEP, RAY_PARAM_COUNT)[:, :FC].astype(jnp.bfloat16)
        )
    if earlier is not None:
        kept.wait()
    last = pltpu.make_async_copy(stage, out, out_sem.at[0])
    last.start()
    last.wait()


def encode(blocks, table, earlier=None):
    anywhere = pl.BlockSpec(memory_space=pl.ANY)

    def kernel(*refs):
        if earlier is None:
            refs = (*refs[:2], None, *refs[2:])
        encode_kernel(*refs)

    operands = (blocks, table) if earlier is None else (blocks, table, earlier)
    height = FC if earlier is None else FB
    rows = (PAIRS, 2) if blocks.ndim == 4 else (LAYERS * SLAB_SLOTS,)
    return pl.pallas_call(
        kernel,
        in_specs=[anywhere] * len(operands),
        out_specs=anywhere,
        out_shape=jax.ShapeDtypeStruct((SLAB_SLOTS, height, 2 * RAY_PARAM_COUNT), jnp.bfloat16),
        scratch_shapes=[
            pltpu.VMEM((DEVICES, *rows, 128), jnp.bfloat16),
            pltpu.VMEM((FC, SHOTS, 2 * RAY_PARAM_COUNT), jnp.bfloat16),
            pltpu.VMEM((DEVICES, WIDE, 128), jnp.float32),
            pltpu.VMEM((UNIT, FC * TALL, 128), jnp.float32),
            pltpu.VMEM((2, SLAB_SLOTS * DEEP, RAY_PARAM_COUNT), jnp.float32),
            pltpu.VMEM((SLAB_SLOTS, height, 2 * RAY_PARAM_COUNT), jnp.bfloat16),
            pltpu.SemaphoreType.DMA((LAYERS * PARTS,)),
            pltpu.SemaphoreType.DMA((FC // GROUP,)),
            pltpu.SemaphoreType.DMA((2,)),
        ],
        compiler_params=pltpu.CompilerParams(vmem_limit_bytes=LIMIT),
    )(*operands)


def on_device(traces, trace_counts, aperture_start, shot_position, rec_slot):
    own = (trace_counts, aperture_start, shot_position, rec_slot)
    everyone = ("freq", "slab")
    first = lax.all_to_all(spread(0, traces, *own), everyone, split_axis=0, concat_axis=0, tiled=True)
    second = lax.all_to_all(spread(1, traces, *own), everyone, split_axis=0, concat_axis=0, tiled=True)
    note = first[:, PAIRS, 0, : 2 * UNIT].astype(jnp.int32)
    positions = (note[:, :UNIT] * 64 + note[:, UNIT:]).T.reshape(LAYERS, SIDE, DEVICES)
    turn = lax.rem(SIDE - lax.rem(lax.axis_index("freq"), SIDE), SIDE)
    positions = lax.dynamic_slice_in_dim(jnp.concatenate([positions, positions], axis=1), turn, SIDE, axis=1)
    positions = jnp.broadcast_to(positions.reshape(SHOTS, 1), (SHOTS, RAY_PARAM_COUNT))
    first_bin = (F0 + lax.axis_index("freq") * FB).astype(jnp.int32).reshape(1)
    low = encode(first, phases(first_bin, positions))
    return encode(second, phases(first_bin + FC, positions), low)


def solution(mesh):
    return jax.shard_map(
        on_device,
        mesh=mesh,
        in_specs=(
            P(("freq", "slab"), None),
            P(("freq", "slab"), None),
            P(("freq", "slab")),
            P(("freq", "slab")),
            P(),
        ),
        out_specs=P("slab", "freq", None),
        check_vma=False,
    )
```

```python
import math

import jax
import jax.numpy as jnp
import ml_dtypes
import numpy as np
from jax import lax
from jax.experimental import pallas as pl
from jax.experimental.pallas import tpu as pltpu
from jax.sharding import PartitionSpec as P

NT = 2048
FREQUENCY_COUNT = 256
F0 = 8
RAY_PARAM_COUNT = 128
NREC = 512
RDIV = 16
SLAB_SLOTS = 48
ROWS = 3072
UNIT = 8
FREQ_DEV = 8
SLAB_DEV = 16
DEVICES = FREQ_DEV * SLAB_DEV
SLOTS = SLAB_SLOTS * SLAB_DEV
FB = FREQUENCY_COUNT // FREQ_DEV
PASSES = 2
FC = FB // PASSES
VALUES = 2 * FC * FREQ_DEV
SPAN = 2 * FC
SIDE = 128 // SPAN
LAYERS = UNIT // SIDE
PAIRS = LAYERS * SLAB_SLOTS // 2
NOTE_ROWS = 2
SHOTS = UNIT * DEVICES
DFT_ROWS = 768
WINDOW = NREC + 256
DFT_STEPS = ROWS // DFT_ROWS
AHEAD = 2
LIMIT = 60 * 2**20


def dft_table(part):
    column = np.arange(VALUES)
    owner, within = column // SPAN, column % SPAN
    bins = F0 + owner * FB + part * FC + within % FC
    angle = (np.arange(NT)[:, None] * bins[None, :] % NT) * (2.0 * math.pi / NT)
    factor = 1.0 / math.sqrt(NT)
    table = np.where((within // FC == 0)[None, :], np.cos(angle), -np.sin(angle)) * factor
    return table.astype(np.float32).astype(ml_dtypes.bfloat16)


def spread_kernel(counts, starts, positions, rec_slot, traces, table, out, rows_in, factors, names, spectra, placed, stage, in_sem, out_sem):
    noted = len(stage.shape) == 4

    def rows_copy(i):
        at = pl.ds(pl.multiple_of(i * DFT_ROWS, DFT_ROWS), DFT_ROWS)
        return pltpu.make_async_copy(traces.at[at], rows_in.at[at], in_sem.at[i])

    def owner_copy(owner):
        at = pl.ds(owner * SLAB_DEV, SLAB_DEV)
        return pltpu.make_async_copy(stage.at[at], out.at[at], out_sem.at[owner])

    table_copy = pltpu.make_async_copy(table, factors, in_sem.at[DFT_STEPS])
    table_copy.start()
    for i in range(AHEAD):
        rows_copy(i).start()
    spectra[...] = jnp.zeros(spectra.shape, jnp.bfloat16)
    if noted:
        lane = lax.broadcasted_iota(jnp.int32, (1, 1, NOTE_ROWS, 128), 3)
        note = jnp.zeros((1, 1, NOTE_ROWS, 128), jnp.int32)
        for k in range(UNIT):
            x = positions[k]
            note = jnp.where(lane == k, x // 64, note)
            note = jnp.where(lane == UNIT + k, lax.rem(x, 64), note)
        note = note.astype(jnp.float32).astype(jnp.bfloat16)
        stage[:, PAIRS:] = jnp.broadcast_to(note, (DEVICES, 1, NOTE_ROWS, 128))
    begin = jnp.int32(0)
    lane = lax.broadcasted_iota(jnp.int32, (1, WINDOW), 1)
    for k in range(UNIT):
        skip = lax.rem(begin, 16)
        shift = lax.rem(skip - starts[k] + NREC, NREC)
        slots = pltpu.roll(jnp.broadcast_to(rec_slot[...], (8, NREC)), shift, 1)[:1]
        slots = jnp.concatenate([slots, slots[:, : WINDOW - NREC]], axis=1)
        names[k : k + 1, :] = jnp.where((lane >= skip) & (lane < skip + counts[0, k]), slots, -1)
        begin = begin + counts[0, k]
    table_copy.wait()
    group = lax.broadcasted_iota(jnp.int32, (SLOTS, 128), 1) // SPAN

    def join(layer):
        height = (SLAB_SLOTS // 2, 2) if noted else (SLAB_SLOTS,)
        at = pl.ds(layer * height[0] if noted else pl.multiple_of(layer * SLAB_SLOTS, 16), height[0])
        for tile in range(VALUES // 128):
            pieces = [placed[side, :, tile * 128 : tile * 128 + 128] for side in range(SIDE)]
            for k in range(SIDE):
                joined = pieces[(SIDE - 1 - k) % SIDE]
                for g in range(SIDE - 1):
                    joined = jnp.where(group == g, pieces[(g - k) % SIDE], joined)
                owner = tile * SIDE + k
                stage[owner * SLAB_DEV : (owner + 1) * SLAB_DEV, at] = joined.astype(jnp.bfloat16).reshape(
                    SLAB_DEV, *height, 128
                )

                @pl.when(layer == LAYERS - 1)
                def _():
                    owner_copy(owner).start()

    def place(carry):
        shot, begin = carry
        side = lax.rem(shot, SIDE)
        count = counts[0, shot]
        base = pl.multiple_of((begin // 16) * 16, 16)
        skip = begin - base

        def product(depth):
            name = names[pl.ds(shot, 1), :depth]
            onehot = (lax.broadcasted_iota(jnp.int32, (SLOTS, depth), 0) == name).astype(jnp.float32)
            found = jnp.dot(
                onehot.astype(jnp.bfloat16),
                spectra[pl.ds(base, depth), :],
                preferred_element_type=jnp.float32,
            )
            for tile in range(VALUES // 128):
                lanes = slice(tile * 128, tile * 128 + 128)
                placed[side, :, lanes] = pltpu.roll(found[:, lanes], side * SPAN, 1)

        small = skip + count <= NREC

        @pl.when(small)
        def _():
            product(NREC)

        @pl.when(jnp.logical_not(small))
        def _():
            product(WINDOW)

        @pl.when(side == SIDE - 1)
        def _():
            join(shot // SIDE)

        return shot + 1, begin + count

    def block(i, carry):
        rows_copy(i).wait()

        @pl.when(i + AHEAD < DFT_STEPS)
        def _():
            rows_copy(i + AHEAD).start()

        at = pl.ds(pl.multiple_of(i * DFT_ROWS, DFT_ROWS), DFT_ROWS)
        spectra[at, :] = jnp.dot(
            rows_in[at, :], factors[...], preferred_element_type=jnp.float32
        ).astype(jnp.bfloat16)
        have = (i + 1) * DFT_ROWS

        def ready(carry):
            shot, begin = carry
            return (shot < UNIT) & (begin + counts[0, jnp.minimum(shot, UNIT - 1)] <= have)

        return lax.while_loop(ready, place, carry)

    lax.fori_loop(0, DFT_STEPS, block, (jnp.int32(0), jnp.int32(0)))
    for owner in range(FREQ_DEV):
        owner_copy(owner).wait()


def spread(part, traces, counts, starts, positions, rec_slot):
    rows = (PAIRS + 1, 2) if part == 0 else (LAYERS * SLAB_SLOTS,)
    scalars = pl.BlockSpec(memory_space=pltpu.SMEM)
    anywhere = pl.BlockSpec(memory_space=pl.ANY)
    return pl.pallas_call(
        spread_kernel,
        in_specs=[scalars, scalars, scalars, pl.BlockSpec(memory_space=pltpu.VMEM), anywhere, anywhere],
        out_specs=anywhere,
        out_shape=jax.ShapeDtypeStruct((DEVICES, *rows, 128), jnp.bfloat16),
        scratch_shapes=[
            pltpu.VMEM((ROWS, NT), jnp.bfloat16),
            pltpu.VMEM((NT, VALUES), jnp.bfloat16),
            pltpu.VMEM((UNIT, WINDOW), jnp.int32),
            pltpu.VMEM((ROWS + WINDOW, VALUES), jnp.bfloat16),
            pltpu.VMEM((SIDE, SLOTS, VALUES), jnp.float32),
            pltpu.VMEM((DEVICES, *rows, 128), jnp.bfloat16),
            pltpu.SemaphoreType.DMA((DFT_STEPS + 1,)),
            pltpu.SemaphoreType.DMA((FREQ_DEV,)),
        ],
        compiler_params=pltpu.CompilerParams(vmem_limit_bytes=LIMIT),
    )(counts, starts, positions, rec_slot.reshape(1, NREC), traces, jnp.asarray(dft_table(part)))


PHASE_ROWS = 128


def phase_kernel(first_bin, positions, out):
    period = NT * RDIV
    unit = 2.0 * math.pi / period
    scale = 1.0 / math.sqrt(SHOTS)
    tile = 16
    ray = lax.broadcasted_iota(jnp.int32, (tile, RAY_PARAM_COUNT), 1) - RAY_PARAM_COUNT // 2

    def turn(k):
        centred = ((k + period // 2) & (period - 1)) - period // 2
        angle = centred.astype(jnp.float32) * unit
        return jnp.cos(angle), jnp.sin(angle)

    def body(t, carry):
        rows = pl.multiple_of(t * tile, tile)
        delay = positions[pl.ds(rows, tile), :] * ray
        step_cos, step_sin = turn(delay)
        c, s = turn(delay * first_bin[0])
        c, s = c * scale, s * scale
        for f in range(FC):
            out[f, pl.ds(rows, tile), :RAY_PARAM_COUNT] = c.astype(jnp.bfloat16)
            out[f, pl.ds(rows, tile), RAY_PARAM_COUNT:] = s.astype(jnp.bfloat16)
            c, s = c * step_cos - s * step_sin, s * step_cos + c * step_sin
        return carry

    lax.fori_loop(0, PHASE_ROWS // tile, body, 0)


def phases(first_bin, positions):
    return pl.pallas_call(
        phase_kernel,
        grid=(SHOTS // PHASE_ROWS,),
        in_specs=[
            pl.BlockSpec(memory_space=pltpu.SMEM),
            pl.BlockSpec((PHASE_ROWS, RAY_PARAM_COUNT), lambda i: (i, 0)),
        ],
        out_specs=pl.BlockSpec((FC, PHASE_ROWS, 2 * RAY_PARAM_COUNT), lambda i: (0, i, 0)),
        out_shape=jax.ShapeDtypeStruct((FC, SHOTS, 2 * RAY_PARAM_COUNT), jnp.bfloat16),
        compiler_params=pltpu.CompilerParams(vmem_limit_bytes=LIMIT),
    )(first_bin, positions)


PART = 16
PARTS = SLAB_SLOTS // PART
WIDE = PART + 8
LANES = 2 * SLAB_SLOTS
TALL = LANES + 8
DEEP = FC + 8
GROUP = 4


def encode_kernel(blocks, table, earlier, out, raw, factors, wide, lattice, encoded, stage, in_sem, table_sem, out_sem):
    def part_rows(p):
        if len(raw.shape) == 4:
            return pl.ds(p * (PART // 2), PART // 2)
        return pl.ds(pl.multiple_of(p * PART, PART), PART)

    def part_copy(p):
        at = part_rows(p)
        return pltpu.make_async_copy(blocks.at[:, at], raw.at[:, at], in_sem.at[p])

    def table_copy(g):
        at = pl.ds(g * GROUP, GROUP)
        return pltpu.make_async_copy(table.at[at], factors.at[at], table_sem.at[g])

    for p in range(LAYERS * PARTS):
        part_copy(p).start()
    if earlier is not None:
        kept = pltpu.make_async_copy(earlier, stage.at[:, :FC], out_sem.at[1])
        kept.start()
    flat = wide.reshape(DEVICES * WIDE, 128)

    def turn(p, carry):
        part_copy(p).wait()

        @pl.when(p == 0)
        def _():
            for g in range(FC // GROUP):
                table_copy(g).start()

        layer, part = p // PARTS, lax.rem(p, PARTS)
        wide[:, :PART] = raw[:, part_rows(p)].reshape(DEVICES, PART, 128).astype(jnp.float32)
        for s in range(PART):
            turned = jnp.transpose(flat[pl.ds(s, DEVICES, stride=WIDE), :].astype(jnp.bfloat16)).astype(jnp.float32)
            for side in range(SIDE):
                for c in range(2):
                    at = side * SPAN + c * FC
                    lattice[
                        layer * SIDE + side, pl.ds(c * SLAB_SLOTS + part * PART + s, FC, stride=TALL), :
                    ] = turned[at : at + FC, :]
        return carry

    lax.fori_loop(0, LAYERS * PARTS, turn, 0)

    def sum_shots(g, carry):
        table_copy(g).wait()
        for k in range(GROUP):
            f = g * GROUP + k
            at = pl.multiple_of(f * TALL, 8)
            rows = jnp.concatenate(
                [lattice[o, pl.ds(at, LANES), :].astype(jnp.bfloat16) for o in range(UNIT)], axis=1
            )
            both = jnp.dot(rows, factors[f], preferred_element_type=jnp.float32)
            re, im = both[:SLAB_SLOTS], both[SLAB_SLOTS:]
            n = RAY_PARAM_COUNT
            encoded[0, pl.ds(f, SLAB_SLOTS, stride=DEEP), :] = re[:, :n] + im[:, n:]
            encoded[1, pl.ds(f, SLAB_SLOTS, stride=DEEP), :] = im[:, :n] - re[:, n:]
        return carry

    lax.fori_loop(0, FC // GROUP, sum_shots, 0)
    own = slice(0, FC) if earlier is None else slice(FC, FB)
    for h in range(2):
        stage[:, own, h * RAY_PARAM_COUNT : (h + 1) * RAY_PARAM_COUNT] = (
            encoded[h].reshape(SLAB_SLOTS, DEEP, RAY_PARAM_COUNT)[:, :FC].astype(jnp.bfloat16)
        )
    if earlier is not None:
        kept.wait()
    last = pltpu.make_async_copy(stage, out, out_sem.at[0])
    last.start()
    last.wait()


def encode(blocks, table, earlier=None):
    anywhere = pl.BlockSpec(memory_space=pl.ANY)

    def kernel(*refs):
        if earlier is None:
            refs = (*refs[:2], None, *refs[2:])
        encode_kernel(*refs)

    operands = (blocks, table) if earlier is None else (blocks, table, earlier)
    height = FC if earlier is None else FB
    rows = (PAIRS, 2) if blocks.ndim == 4 else (LAYERS * SLAB_SLOTS,)
    return pl.pallas_call(
        kernel,
        in_specs=[anywhere] * len(operands),
        out_specs=anywhere,
        out_shape=jax.ShapeDtypeStruct((SLAB_SLOTS, height, 2 * RAY_PARAM_COUNT), jnp.bfloat16),
        scratch_shapes=[
            pltpu.VMEM((DEVICES, *rows, 128), jnp.bfloat16),
            pltpu.VMEM((FC, SHOTS, 2 * RAY_PARAM_COUNT), jnp.bfloat16),
            pltpu.VMEM((DEVICES, WIDE, 128), jnp.float32),
            pltpu.VMEM((UNIT, FC * TALL, 128), jnp.float32),
            pltpu.VMEM((2, SLAB_SLOTS * DEEP, RAY_PARAM_COUNT), jnp.float32),
            pltpu.VMEM((SLAB_SLOTS, height, 2 * RAY_PARAM_COUNT), jnp.bfloat16),
            pltpu.SemaphoreType.DMA((LAYERS * PARTS,)),
            pltpu.SemaphoreType.DMA((FC // GROUP,)),
            pltpu.SemaphoreType.DMA((2,)),
        ],
        compiler_params=pltpu.CompilerParams(vmem_limit_bytes=LIMIT),
    )(*operands)


def on_device(traces, trace_counts, aperture_start, shot_position, rec_slot):
    own = (trace_counts, aperture_start, shot_position, rec_slot)
    everyone = ("freq", "slab")
    first = lax.all_to_all(spread(0, traces, *own), everyone, split_axis=0, concat_axis=0, tiled=True)
    second = lax.all_to_all(spread(1, traces, *own), everyone, split_axis=0, concat_axis=0, tiled=True)
    note = first[:, PAIRS, 0, : 2 * UNIT].astype(jnp.int32)
    positions = (note[:, :UNIT] * 64 + note[:, UNIT:]).T.reshape(LAYERS, SIDE, DEVICES)
    turn = lax.rem(SIDE - lax.rem(lax.axis_index("freq"), SIDE), SIDE)
    positions = lax.dynamic_slice_in_dim(jnp.concatenate([positions, positions], axis=1), turn, SIDE, axis=1)
    positions = jnp.broadcast_to(positions.reshape(SHOTS, 1), (SHOTS, RAY_PARAM_COUNT))
    first_bin = (F0 + lax.axis_index("freq") * FB).astype(jnp.int32).reshape(1)
    low = encode(first, phases(first_bin, positions))
    return encode(second, phases(first_bin + FC, positions), low)


def solution(mesh):
    return jax.shard_map(
        on_device,
        mesh=mesh,
        in_specs=(
            P(("freq", "slab"), None),
            P(("freq", "slab"), None),
            P(("freq", "slab")),
            P(("freq", "slab")),
            P(),
        ),
        out_specs=P("slab", "freq", None),
        check_vma=False,
    )
```

```python
import math

import jax
import jax.numpy as jnp
import ml_dtypes
import numpy as np
from jax import lax
from jax.experimental import pallas as pl
from jax.experimental.pallas import tpu as pltpu
from jax.sharding import PartitionSpec as P

NT = 2048
FREQUENCY_COUNT = 256
F0 = 8
RAY_PARAM_COUNT = 128
NREC = 512
RDIV = 16
SLAB_SLOTS = 48
ROWS = 3072
UNIT = 8
FREQ_DEV = 8
SLAB_DEV = 16
DEVICES = FREQ_DEV * SLAB_DEV
SLOTS = SLAB_SLOTS * SLAB_DEV
FB = FREQUENCY_COUNT // FREQ_DEV
PASSES = 2
FC = FB // PASSES
VALUES = 2 * FC * FREQ_DEV
SPAN = 2 * FC
SIDE = 128 // SPAN
LAYERS = UNIT // SIDE
PAIRS = LAYERS * SLAB_SLOTS // 2
NOTE_ROWS = 2
SHOTS = UNIT * DEVICES
DFT_ROWS = 512
WINDOW = NREC + 256
DFT_STEPS = ROWS // DFT_ROWS
AHEAD = 3
LIMIT = 60 * 2**20


def dft_table(part):
    column = np.arange(VALUES)
    owner, within = column // SPAN, column % SPAN
    bins = F0 + owner * FB + part * FC + within % FC
    angle = (np.arange(NT)[:, None] * bins[None, :] % NT) * (2.0 * math.pi / NT)
    factor = 1.0 / math.sqrt(NT)
    table = np.where((within // FC == 0)[None, :], np.cos(angle), -np.sin(angle)) * factor
    return table.astype(np.float32).astype(ml_dtypes.bfloat16)


def spread_kernel(counts, starts, positions, rec_slot, traces, table, out, rows_in, factors, names, spectra, placed, stage, in_sem, out_sem):
    noted = len(stage.shape) == 4

    def rows_copy(i):
        at = pl.ds(pl.multiple_of(i * DFT_ROWS, DFT_ROWS), DFT_ROWS)
        return pltpu.make_async_copy(traces.at[at], rows_in.at[at], in_sem.at[i])

    def owner_copy(owner):
        at = pl.ds(owner * SLAB_DEV, SLAB_DEV)
        return pltpu.make_async_copy(stage.at[at], out.at[at], out_sem.at[owner])

    table_copy = pltpu.make_async_copy(table, factors, in_sem.at[DFT_STEPS])
    table_copy.start()
    for i in range(AHEAD):
        rows_copy(i).start()
    spectra[...] = jnp.zeros(spectra.shape, jnp.bfloat16)
    if noted:
        lane = lax.broadcasted_iota(jnp.int32, (1, 1, NOTE_ROWS, 128), 3)
        note = jnp.zeros((1, 1, NOTE_ROWS, 128), jnp.int32)
        for k in range(UNIT):
            x = positions[k]
            note = jnp.where(lane == k, x // 64, note)
            note = jnp.where(lane == UNIT + k, lax.rem(x, 64), note)
        note = note.astype(jnp.float32).astype(jnp.bfloat16)
        stage[:, PAIRS:] = jnp.broadcast_to(note, (DEVICES, 1, NOTE_ROWS, 128))
    begin = jnp.int32(0)
    lane = lax.broadcasted_iota(jnp.int32, (1, WINDOW), 1)
    for k in range(UNIT):
        skip = lax.rem(begin, 16)
        shift = lax.rem(skip - starts[k] + NREC, NREC)
        slots = pltpu.roll(jnp.broadcast_to(rec_slot[...], (8, NREC)), shift, 1)[:1]
        slots = jnp.concatenate([slots, slots[:, : WINDOW - NREC]], axis=1)
        names[k : k + 1, :] = jnp.where((lane >= skip) & (lane < skip + counts[0, k]), slots, -1)
        begin = begin + counts[0, k]
    table_copy.wait()
    group = lax.broadcasted_iota(jnp.int32, (SLOTS, 128), 1) // SPAN

    def join(layer):
        height = (SLAB_SLOTS // 2, 2) if noted else (SLAB_SLOTS,)
        at = pl.ds(layer * height[0] if noted else pl.multiple_of(layer * SLAB_SLOTS, 16), height[0])
        for tile in range(VALUES // 128):
            pieces = [placed[side, :, tile * 128 : tile * 128 + 128] for side in range(SIDE)]
            pieces = [pltpu.roll(p, side * SPAN, 1) if side else p for side, p in enumerate(pieces)]
            for k in range(SIDE):
                joined = pieces[(SIDE - 1 - k) % SIDE]
                for g in range(SIDE - 1):
                    joined = jnp.where(group == g, pieces[(g - k) % SIDE], joined)
                owner = tile * SIDE + k
                stage[owner * SLAB_DEV : (owner + 1) * SLAB_DEV, at] = joined.astype(jnp.bfloat16).reshape(
                    SLAB_DEV, *height, 128
                )

                @pl.when(layer == LAYERS - 1)
                def _():
                    owner_copy(owner).start()

    def place(carry):
        shot, begin = carry
        side = lax.rem(shot, SIDE)
        count = counts[0, shot]
        base = pl.multiple_of((begin // 16) * 16, 16)
        skip = begin - base

        def product(depth):
            name = names[pl.ds(shot, 1), :depth]
            onehot = (lax.broadcasted_iota(jnp.int32, (SLOTS, depth), 0) == name).astype(jnp.float32)
            found = jnp.dot(
                onehot.astype(jnp.bfloat16),
                spectra[pl.ds(base, depth), :],
                preferred_element_type=jnp.float32,
            )
            for tile in range(VALUES // 128):
                lanes = slice(tile * 128, tile * 128 + 128)
                placed[side, :, lanes] = found[:, lanes]

        small = skip + count <= NREC

        @pl.when(small)
        def _():
            product(NREC)

        @pl.when(jnp.logical_not(small))
        def _():
            product(WINDOW)

        @pl.when(side == SIDE - 1)
        def _():
            join(shot // SIDE)

        return shot + 1, begin + count

    def block(i, carry):
        rows_copy(i).wait()

        @pl.when(i + AHEAD < DFT_STEPS)
        def _():
            rows_copy(i + AHEAD).start()

        at = pl.ds(pl.multiple_of(i * DFT_ROWS, DFT_ROWS), DFT_ROWS)
        spectra[at, :] = jnp.dot(
            rows_in[at, :], factors[...], preferred_element_type=jnp.float32
        ).astype(jnp.bfloat16)
        have = (i + 1) * DFT_ROWS

        def ready(carry):
            shot, begin = carry
            return (shot < UNIT) & (begin + counts[0, jnp.minimum(shot, UNIT - 1)] <= have)

        return lax.while_loop(ready, place, carry)

    lax.fori_loop(0, DFT_STEPS, block, (jnp.int32(0), jnp.int32(0)))
    for owner in range(FREQ_DEV):
        owner_copy(owner).wait()


def spread(part, traces, counts, starts, positions, rec_slot):
    rows = (PAIRS + 1, 2) if part == 0 else (LAYERS * SLAB_SLOTS,)
    scalars = pl.BlockSpec(memory_space=pltpu.SMEM)
    anywhere = pl.BlockSpec(memory_space=pl.ANY)
    return pl.pallas_call(
        spread_kernel,
        in_specs=[scalars, scalars, scalars, pl.BlockSpec(memory_space=pltpu.VMEM), anywhere, anywhere],
        out_specs=anywhere,
        out_shape=jax.ShapeDtypeStruct((DEVICES, *rows, 128), jnp.bfloat16),
        scratch_shapes=[
            pltpu.VMEM((ROWS, NT), jnp.bfloat16),
            pltpu.VMEM((NT, VALUES), jnp.bfloat16),
            pltpu.VMEM((UNIT, WINDOW), jnp.int32),
            pltpu.VMEM((ROWS + WINDOW, VALUES), jnp.bfloat16),
            pltpu.VMEM((SIDE, SLOTS, VALUES), jnp.float32),
            pltpu.VMEM((DEVICES, *rows, 128), jnp.bfloat16),
            pltpu.SemaphoreType.DMA((DFT_STEPS + 1,)),
            pltpu.SemaphoreType.DMA((FREQ_DEV,)),
        ],
        compiler_params=pltpu.CompilerParams(vmem_limit_bytes=LIMIT),
    )(counts, starts, positions, rec_slot.reshape(1, NREC), traces, jnp.asarray(dft_table(part)))


PHASE_ROWS = 128


def phase_kernel(first_bin, positions, out):
    period = NT * RDIV
    unit = 2.0 * math.pi / period
    scale = 1.0 / math.sqrt(SHOTS)
    tile = 16
    ray = lax.broadcasted_iota(jnp.int32, (tile, RAY_PARAM_COUNT), 1) - RAY_PARAM_COUNT // 2

    def turn(k):
        centred = ((k + period // 2) & (period - 1)) - period // 2
        angle = centred.astype(jnp.float32) * unit
        return jnp.cos(angle), jnp.sin(angle)

    def body(t, carry):
        rows = pl.multiple_of(t * tile, tile)
        delay = positions[pl.ds(rows, tile), :] * ray
        step_cos, step_sin = turn(delay)
        c, s = turn(delay * first_bin[0])
        c, s = c * scale, s * scale
        for f in range(FC):
            out[f, pl.ds(rows, tile), :RAY_PARAM_COUNT] = c.astype(jnp.bfloat16)
            out[f, pl.ds(rows, tile), RAY_PARAM_COUNT:] = s.astype(jnp.bfloat16)
            c, s = c * step_cos - s * step_sin, s * step_cos + c * step_sin
        return carry

    lax.fori_loop(0, PHASE_ROWS // tile, body, 0)


def phases(first_bin, positions):
    return pl.pallas_call(
        phase_kernel,
        grid=(SHOTS // PHASE_ROWS,),
        in_specs=[
            pl.BlockSpec(memory_space=pltpu.SMEM),
            pl.BlockSpec((PHASE_ROWS, RAY_PARAM_COUNT), lambda i: (i, 0)),
        ],
        out_specs=pl.BlockSpec((FC, PHASE_ROWS, 2 * RAY_PARAM_COUNT), lambda i: (0, i, 0)),
        out_shape=jax.ShapeDtypeStruct((FC, SHOTS, 2 * RAY_PARAM_COUNT), jnp.bfloat16),
        compiler_params=pltpu.CompilerParams(vmem_limit_bytes=LIMIT),
    )(first_bin, positions)


PART = 16
PARTS = SLAB_SLOTS // PART
WIDE = PART + 8
LANES = 2 * SLAB_SLOTS
TALL = LANES + 8
DEEP = FC + 8
GROUP = 4


def encode_kernel(blocks, table, earlier, out, raw, factors, wide, lattice, encoded, stage, in_sem, table_sem, out_sem):
    def part_rows(p):
        if len(raw.shape) == 4:
            return pl.ds(p * (PART // 2), PART // 2)
        return pl.ds(pl.multiple_of(p * PART, PART), PART)

    def part_copy(p):
        at = part_rows(p)
        return pltpu.make_async_copy(blocks.at[:, at], raw.at[:, at], in_sem.at[p])

    def table_copy(g):
        at = pl.ds(g * GROUP, GROUP)
        return pltpu.make_async_copy(table.at[at], factors.at[at], table_sem.at[g])

    for p in range(LAYERS * PARTS):
        part_copy(p).start()
    if earlier is not None:
        kept = pltpu.make_async_copy(earlier, stage.at[:, :FC], out_sem.at[1])
        kept.start()
    flat = wide.reshape(DEVICES * WIDE, 128)

    def turn(p, carry):
        part_copy(p).wait()

        @pl.when(p == 0)
        def _():
            for g in range(FC // GROUP):
                table_copy(g).start()

        layer, part = p // PARTS, lax.rem(p, PARTS)
        wide[:, :PART] = raw[:, part_rows(p)].reshape(DEVICES, PART, 128).astype(jnp.float32)
        for s in range(PART):
            turned = jnp.transpose(flat[pl.ds(s, DEVICES, stride=WIDE), :].astype(jnp.bfloat16)).astype(jnp.float32)
            for side in range(SIDE):
                for c in range(2):
                    at = side * SPAN + c * FC
                    lattice[
                        layer * SIDE + side, pl.ds(c * SLAB_SLOTS + part * PART + s, FC, stride=TALL), :
                    ] = turned[at : at + FC, :]
        return carry

    lax.fori_loop(0, LAYERS * PARTS, turn, 0)

    def sum_shots(g, carry):
        table_copy(g).wait()
        for k in range(GROUP):
            f = g * GROUP + k
            at = pl.multiple_of(f * TALL, 8)
            rows = jnp.concatenate(
                [lattice[o, pl.ds(at, LANES), :].astype(jnp.bfloat16) for o in range(UNIT)], axis=1
            )
            both = jnp.dot(rows, factors[f], preferred_element_type=jnp.float32)
            re, im = both[:SLAB_SLOTS], both[SLAB_SLOTS:]
            n = RAY_PARAM_COUNT
            encoded[0, pl.ds(f, SLAB_SLOTS, stride=DEEP), :] = re[:, :n] + im[:, n:]
            encoded[1, pl.ds(f, SLAB_SLOTS, stride=DEEP), :] = im[:, :n] - re[:, n:]
        return carry

    lax.fori_loop(0, FC // GROUP, sum_shots, 0)
    own = slice(0, FC) if earlier is None else slice(FC, FB)
    for h in range(2):
        stage[:, own, h * RAY_PARAM_COUNT : (h + 1) * RAY_PARAM_COUNT] = (
            encoded[h].reshape(SLAB_SLOTS, DEEP, RAY_PARAM_COUNT)[:, :FC].astype(jnp.bfloat16)
        )
    if earlier is not None:
        kept.wait()
    last = pltpu.make_async_copy(stage, out, out_sem.at[0])
    last.start()
    last.wait()


def encode(blocks, table, earlier=None):
    anywhere = pl.BlockSpec(memory_space=pl.ANY)

    def kernel(*refs):
        if earlier is None:
            refs = (*refs[:2], None, *refs[2:])
        encode_kernel(*refs)

    operands = (blocks, table) if earlier is None else (blocks, table, earlier)
    height = FC if earlier is None else FB
    rows = (PAIRS, 2) if blocks.ndim == 4 else (LAYERS * SLAB_SLOTS,)
    return pl.pallas_call(
        kernel,
        in_specs=[anywhere] * len(operands),
        out_specs=anywhere,
        out_shape=jax.ShapeDtypeStruct((SLAB_SLOTS, height, 2 * RAY_PARAM_COUNT), jnp.bfloat16),
        scratch_shapes=[
            pltpu.VMEM((DEVICES, *rows, 128), jnp.bfloat16),
            pltpu.VMEM((FC, SHOTS, 2 * RAY_PARAM_COUNT), jnp.bfloat16),
            pltpu.VMEM((DEVICES, WIDE, 128), jnp.float32),
            pltpu.VMEM((UNIT, FC * TALL, 128), jnp.float32),
            pltpu.VMEM((2, SLAB_SLOTS * DEEP, RAY_PARAM_COUNT), jnp.float32),
            pltpu.VMEM((SLAB_SLOTS, height, 2 * RAY_PARAM_COUNT), jnp.bfloat16),
            pltpu.SemaphoreType.DMA((LAYERS * PARTS,)),
            pltpu.SemaphoreType.DMA((FC // GROUP,)),
            pltpu.SemaphoreType.DMA((2,)),
        ],
        compiler_params=pltpu.CompilerParams(vmem_limit_bytes=LIMIT),
    )(*operands)


def on_device(traces, trace_counts, aperture_start, shot_position, rec_slot):
    own = (trace_counts, aperture_start, shot_position, rec_slot)
    everyone = ("freq", "slab")
    first = lax.all_to_all(spread(0, traces, *own), everyone, split_axis=0, concat_axis=0, tiled=True)
    second = lax.all_to_all(spread(1, traces, *own), everyone, split_axis=0, concat_axis=0, tiled=True)
    note = first[:, PAIRS, 0, : 2 * UNIT].astype(jnp.int32)
    positions = (note[:, :UNIT] * 64 + note[:, UNIT:]).T.reshape(LAYERS, SIDE, DEVICES)
    turn = lax.rem(SIDE - lax.rem(lax.axis_index("freq"), SIDE), SIDE)
    positions = lax.dynamic_slice_in_dim(jnp.concatenate([positions, positions], axis=1), turn, SIDE, axis=1)
    positions = jnp.broadcast_to(positions.reshape(SHOTS, 1), (SHOTS, RAY_PARAM_COUNT))
    first_bin = (F0 + lax.axis_index("freq") * FB).astype(jnp.int32).reshape(1)
    low = encode(first, phases(first_bin, positions))
    return encode(second, phases(first_bin + FC, positions), low)


def solution(mesh):
    return jax.shard_map(
        on_device,
        mesh=mesh,
        in_specs=(
            P(("freq", "slab"), None),
            P(("freq", "slab"), None),
            P(("freq", "slab")),
            P(("freq", "slab")),
            P(),
        ),
        out_specs=P("slab", "freq", None),
        check_vma=False,
    )
```
